768 devices in a mesh: blk: 96 (over y_lo, z, core), grp: 8 (over y_hi, x).
Axes of the slice: x: 4, y: 8 (y_hi: 2, y_lo: 4; y = y_hi * 4 + y_lo), z: 12, core: 2. Of those that a mesh axis runs over, the one named last changes fastest.
Arguments:
- three_index: bfloat16 [23552, 24576], P('grp', 'blk'), may hold values from -0.359375 to 0.359375
- occ_energy: float32 [384], P('blk'), may hold values from -2 to -0.3
- vir_energy: float32 [64], replicated, may hold values from 0.2 to 3
- aux_count: int32 [8], replicated, may hold values from 1 to 2944, 22528 in all
- occ_count: int32 [96], replicated, may hold values from 1 to 4, 192 in all
Outputs:
- gamma: bfloat16 [23552, 24576], P('grp', 'blk')
The draws below stay inside these ranges and needn't reach their ends.
Inputs may be any that keep to these rules, and one draw needn't show every extreme that they name: `aux_count`: the 8 counts sum to 22528; the largest is exactly 2944. `occ_count`: the 96 counts sum to 192; the largest is exactly 4.
All inputs are finite; a program needn't handle non-finite values.
Results may differ from the reference program's by a relative error of at most 0.018.
Values may be sent and summed in bfloat16 or wider, within the bound.
No kernel may reach another device: no remote copies, remote signals or barrier semaphores. Data moves between devices by JAX's collectives and lax.ppermute only.
A program may use at most 32 MiB of HBM per device.

```python
import math
import jax
import jax.numpy as jnp
import numpy as np
from jax import lax

NAUX = 22528
NV = 64
OCC_CAP = 4
NOCC = 192
NOCC_PAD = 384
CAP = 2944
SLOTS = 23552
COLS = 24576
N_BLK = 96
N_GRP = 8


def levels(rng, extent, pieces, smallest, top_value):
    gain, own = 1.0, jax.random.fold_in(rng, 6)
    for dim, shards_of in pieces:
        heights = jnp.exp(jax.random.uniform(jax.random.fold_in(own, dim), (shards_of,), jnp.float32, smallest / len(pieces), top_value / len(pieces)))
        gain = gain * jnp.repeat(heights, extent[dim] // shards_of).reshape([-1 if axis == dim else 1 for axis in range(len(extent))])
    return gain


def length_profile(amount, total, bound, lean):
    weights = [(1 << 20) // math.isqrt(grade ** lean) + 1 for grade in range(2, amount + 1)]
    surplus, given = total - bound - (amount - 1), [1] * (amount - 1)
    while surplus > 0:
        candidates = [i for i in range(amount - 1) if given[i] < bound]
        whole, left = sum([weights[i] for i in candidates]), surplus
        for i in candidates:
            extra = min(bound - given[i], max(1, left * weights[i] // whole), surplus)
            given[i] = given[i] + extra
            surplus = surplus - extra
    return np.array([bound] + given)


def uneven_parts(own_key, count, total, limit, lean):
    if count == 2:
        one = jax.random.randint(own_key, (), max(1, total - limit), min(limit, total - 1) + 1)
        return jnp.stack([one, total - one])
    lengths = jnp.asarray(length_profile(count, total, limit, lean), jnp.int32)
    couples = (count - 1) // 2
    donor, receiver = lengths[1:1 + 2 * couples:2], lengths[2:2 + 2 * couples:2]
    room = jnp.minimum(donor - 1, limit - receiver)
    shifted = jax.random.randint(jax.random.fold_in(own_key, 1), (couples,), 0, 1 << 20) % (room + 1)
    lengths = lengths.at[1:1 + 2 * couples:2].set(donor - shifted).at[2:2 + 2 * couples:2].set(receiver + shifted)
    return lengths[jax.random.permutation(jax.random.fold_in(own_key, 2), count)]


def normal_values(own_key, shape, scale, reach, split=(), held_as=jnp.bfloat16):
    drawn = jax.random.normal(own_key, shape, jnp.float32) * scale
    if len(split) > 0:
        drawn = levels(own_key, shape, split, -0.22, 0.18) * drawn
    return jnp.clip(drawn, min=-reach, max=reach).astype(held_as)


def setup_inputs(seed: int = 0) -> dict:
    keys = jax.random.split(jax.random.key(seed), 6)
    return {
        "three_index": normal_values(keys[0], (SLOTS, COLS), 0.06, 0.359375, ((0, 8), (1, 96))),
        "occ_energy": jnp.clip(-2.0 + 1.7 * jax.random.uniform(keys[1], (NOCC_PAD,), jnp.float32) ** levels(keys[1], (NOCC_PAD,), ((0, 96),), -0.2, 0.2), -2.0, -0.3),
        "vir_energy": jnp.clip(jax.random.uniform(keys[2], (NV,), jnp.float32, 0.2, 3.0), 0.2, 3.0),
        "aux_count": uneven_parts(keys[3], N_GRP, NAUX, CAP, 2).astype(jnp.int32),
        "occ_count": uneven_parts(keys[4], N_BLK, NOCC, OCC_CAP, 2).astype(jnp.int32),
    }


contract_first = (((0,), (0,)), ((), ()))
contract_last = (((1,), (1,)), ((), ()))


def slab_parts(masked, occ_energy, vir_energy, occ_count, slab_index):
    columns = OCC_CAP * NV
    slab_block = lax.dynamic_slice_in_dim(masked, slab_index * columns, columns, 1).astype(jnp.float32)
    slab_energy = lax.dynamic_slice_in_dim(occ_energy, slab_index * OCC_CAP, OCC_CAP, 0)
    col_gap = (slab_energy[:, None] - vir_energy[None, :]).reshape(columns)
    col_live = jnp.repeat(jnp.arange(OCC_CAP) < occ_count[slab_index], NV)
    return slab_block, col_gap, col_live


def amplitude_block(left_parts, right_parts):
    pair_block = lax.dot_general(left_parts[0], right_parts[0], contract_first, precision=lax.Precision.HIGHEST)
    quotient = pair_block / (left_parts[1][:, None] + right_parts[1][None, :])
    both_live = left_parts[2][:, None] & right_parts[2][None, :]
    return jnp.where(both_live, quotient, 0.0).astype(jnp.bfloat16)


def reference(three_index, occ_energy, vir_energy, aux_count, occ_count):
    slot_count = three_index.shape[0] // N_GRP
    aux_live = (jnp.arange(slot_count)[None, :] < aux_count[:, None]).reshape(-1)
    masked = jnp.where(aux_live[:, None], three_index, jnp.zeros((), jnp.bfloat16))

    def slab_of(slab_index):
        return slab_parts(masked, occ_energy, vir_energy, occ_count, slab_index % N_BLK)

    def pair_blocks(slab_index):
        left_parts = slab_of(slab_index)
        return jnp.stack([amplitude_block(left_parts, slab_of(slab_index + offset)) for offset in range(3)])

    slab_ids = jnp.arange(N_BLK, dtype=jnp.int32)
    amplitude = lax.map(pair_blocks, slab_ids)

    def collect_slab(slab_index):
        accumulated = jnp.zeros((masked.shape[0], OCC_CAP * NV), jnp.float32)
        for offset in range(3):
            right_slab = slab_of(slab_index + offset)[0]
            accumulated = accumulated + lax.dot_general(right_slab, amplitude[slab_index, offset].astype(jnp.float32), contract_last, precision=lax.Precision.HIGHEST)
        for offset in (1, 2):
            source = (slab_index - offset) % N_BLK
            left_slab = slab_of(source)[0]
            returned = jnp.dot(left_slab, amplitude[source, offset].astype(jnp.float32), precision=lax.Precision.HIGHEST).astype(jnp.bfloat16)
            accumulated = accumulated + lax.optimization_barrier(returned).astype(jnp.float32)
        return accumulated.astype(jnp.bfloat16)

    gamma = lax.map(collect_slab, slab_ids)
    return jnp.transpose(gamma, (1, 0, 2)).reshape(masked.shape[0], N_BLK * OCC_CAP * NV)
```

```python
import jax
import jax.numpy as jnp
from jax import lax
from jax.experimental import pallas as pl
from jax.experimental.pallas import tpu as pltpu
from jax.sharding import PartitionSpec as P


BF = jnp.bfloat16
F32 = jnp.float32
first = (((0,), (0,)), ((), ()))
last = (((1,), (1,)), ((), ()))


def dot0(a, b):
    return lax.dot_general(a, b, first, preferred_element_type=F32)


def keep_rows(block, start, count):
    row = lax.broadcasted_iota(jnp.int32, block.shape, 0) + start
    return jnp.where(row < count, block, jnp.zeros((), block.dtype))


def near_kernel(sc, o_ref, p_ref, out_ref, acc):
    step = pl.program_id(0)
    tile = o_ref.shape[0]

    @pl.when(step == 0)
    def _():
        acc[...] = jnp.zeros_like(acc)

    own = keep_rows(o_ref[...], step * tile, sc[0])
    acc[0] += dot0(own, own)
    acc[1] += dot0(p_ref[...], own)

    @pl.when(step == pl.num_programs(0) - 1)
    def _():
        for j in range(2):
            out_ref[:, j] = acc[j].reshape(out_ref.shape[0], *out_ref.shape[2:]).astype(BF)


def far_kernel(half, sc, n_ref, m_ref, o0_ref, o1_ref, p0_ref, p1_ref, out_ref, acc):
    step = pl.program_id(0)
    tile = n_ref.shape[0]

    @pl.when(step == 0)
    def _():
        acc[...] = jnp.zeros_like(acc)

    own0 = keep_rows(o0_ref[...], step * tile, sc[0])
    own1 = keep_rows(o1_ref[...], half + step * tile, sc[0])
    acc[0] += dot0(n_ref[...], own0)
    acc[1] += dot0(own1, m_ref[...])

    @pl.when(sc[1] == 0)
    def _():
        acc[2] += dot0(n_ref[...], keep_rows(p0_ref[...], step * tile, sc[0]))

    @pl.when(sc[1] == 1)
    def _():
        acc[2] += dot0(keep_rows(p1_ref[...], half + step * tile, sc[0]), m_ref[...])

    @pl.when(step == pl.num_programs(0) - 1)
    def _():
        for j in range(3):
            out_ref[:, j] = acc[j].reshape(out_ref.shape[0], *out_ref.shape[2:]).astype(BF)


def three_terms(value):
    hi = value.astype(BF)
    rest = value - hi.astype(F32)
    mid = rest.astype(BF)
    low = (rest - mid.astype(F32)).astype(BF)
    return hi.astype(F32), mid.astype(F32), low.astype(F32)


def divide(pair, gap_rows, gap_cols, row_live, col_count, vir_count):
    col = lax.broadcasted_iota(jnp.int32, pair.shape, 1)
    keep = (col < col_count * vir_count) & row_live
    return jnp.where(keep, pair / (gap_rows + gap_cols), 0.0).astype(BF)


def near_amplitude_kernel(nv, sc, parts_ref, gaps_ref, vir_ref, out_ref, head_ref):
    total = jnp.sum(parts_ref[...].astype(F32), axis=0)
    vir = vir_ref[...]
    for j in range(2):
        rows = gaps_ref[2 + j:3 + j, :] - vir
        amp = divide(total[j], rows, gaps_ref[0:1, :], sc[2] < sc[3 + j], sc[3], nv)
        for g in range(out_ref.shape[0]):
            out_ref[g, j] = amp
    rows = []
    for j in range(4):
        rows += three_terms(gaps_ref[j:j + 1, :])
    rows.append(jnp.zeros((4, gaps_ref.shape[1]), F32))
    head_ref[...] = jnp.concatenate(rows, axis=0).astype(BF)


def pack_kernel(parts_ref, head_ref, sum_ref, up_ref, down_ref, swap_ref):
    total = jnp.sum(parts_ref[...].astype(F32), axis=0)
    sum_ref[...] = total[:2]
    extra = total[2].astype(BF)
    size = extra.shape[0]
    swap_ref[...] = extra
    for j, ref in ((0, up_ref), (1, down_ref)):
        ref[0:size, :] = total[j].astype(BF)
        ref[size:2 * size, :] = extra
        ref[2 * size:, :] = head_ref[...]


def far_amplitude_kernel(nv, sc, sum_ref, above_ref, below_ref, swap_ref, gaps_ref, vir_ref, out_ref):
    vir = vir_ref[...]
    size = vir.shape[0]
    own_gap = gaps_ref[0:1, :]
    own_rows = gaps_ref[2:3, :] - vir
    copies = range(out_ref.shape[0])

    def head(ref, row):
        block = ref[2 * size:, :].astype(F32)
        return block[3 * row:3 * row + 1] + block[3 * row + 1:3 * row + 2] + block[3 * row + 2:3 * row + 3]

    amp = divide(
        sum_ref[0] + above_ref[0:size, :].astype(F32), head(above_ref, 2) - vir, own_gap,
        sc[2] < sc[5], sc[3], nv,
    )
    for g in copies:
        out_ref[g, 0] = amp
    amp = divide(
        sum_ref[1] + below_ref[0:size, :].astype(F32), own_rows, head(below_ref, 0),
        sc[2] < sc[3], sc[6], nv,
    )
    for g in copies:
        out_ref[g, 1] = amp
    other = swap_ref[...].astype(F32)

    @pl.when(sc[1] == 0)
    def _():
        amp = divide(
            other + below_ref[size:2 * size, :].astype(F32), own_rows, head(below_ref, 1),
            sc[2] < sc[3], sc[7], nv,
        )
        for g in copies:
            out_ref[g, 2] = amp

    @pl.when(sc[1] == 1)
    def _():
        amp = divide(
            other + above_ref[size:2 * size, :].astype(F32), head(above_ref, 3) - vir, own_gap,
            sc[2] < sc[7], sc[3], nv,
        )
        for g in copies:
            out_ref[g, 2] = amp


def gamma_kernel(sc, near_ref, far_ref, o_ref, p_ref, n0_ref, n1_ref, m0_ref, m1_ref, x_ref, out_ref, acc):
    step = pl.program_id(0)
    tile = o_ref.shape[0]
    columns = o_ref.shape[1]

    def amp(ref, j):
        return ref[:, j].reshape(columns, columns)

    def times(block, matrix):
        return jnp.dot(block, matrix, preferred_element_type=F32)

    def times_t(block, matrix):
        return lax.dot_general(block, matrix, last, preferred_element_type=F32)

    acc[...] = times(o_ref[...], amp(near_ref, 0)) + times(p_ref[...], amp(near_ref, 1))
    lower = step < pl.num_programs(0) // 2

    @pl.when(lower)
    def _():
        acc[...] += times(n0_ref[...], amp(far_ref, 0)) + times_t(m0_ref[...], amp(far_ref, 1))

    @pl.when(jnp.logical_not(lower))
    def _():
        acc[...] += times(n1_ref[...], amp(far_ref, 0)) + times_t(m1_ref[...], amp(far_ref, 1))

    @pl.when(sc[1] == 0)
    def _():
        acc[...] += times_t(x_ref[...], amp(far_ref, 2))

    @pl.when(sc[1] == 1)
    def _():
        acc[...] += times(x_ref[...], amp(far_ref, 2))

    out_ref[...] = keep_rows(acc[...], step * tile, sc[0]).astype(out_ref.dtype)


def per_device(three_index, occ_energy, vir_energy, aux_count, occ_count):
    rows, cols = three_index.shape
    half = rows // 2
    nv = vir_energy.shape[0]
    slabs = lax.axis_size("blk")
    owners = lax.axis_size("grp")
    piece = cols // owners
    r = lax.axis_index("blk")
    g = lax.axis_index("grp")
    parity = r % 2

    def shift(value, steps):
        return lax.ppermute(value, "blk", [(i, (i + steps) % slabs) for i in range(slabs)])

    def swap(value):
        return lax.ppermute(value, "blk", [(i, i ^ 1) for i in range(slabs)])

    own = three_index
    n0 = shift(own[:half], -2)
    m1 = shift(own[half:], 2)
    partner = swap(own)
    n1 = shift(own[half:], -2)
    m0 = shift(own[:half], 2)

    partner_energy = swap(occ_energy)
    slot = (g * piece) // nv
    fifth = (r + jnp.where(parity == 0, -1, 1)) % slabs
    sc = jnp.stack([
        aux_count[g], parity, slot, occ_count[r], occ_count[r ^ 1],
        occ_count[(r + 2) % slabs], occ_count[(r - 2) % slabs], occ_count[fifth],
    ]).astype(jnp.int32)
    energies = jnp.stack([occ_energy, partner_energy])
    gap = (energies[:, :, None] - vir_energy[None, None, :]).reshape(2, cols)
    mine = jnp.broadcast_to(lax.dynamic_slice_in_dim(energies, slot, 1, 1), (2, cols))
    gaps = jnp.concatenate([gap, mine, jnp.zeros((4, cols), F32)], axis=0)
    vir = jnp.broadcast_to(
        lax.dynamic_slice_in_dim(vir_energy, (g * piece) % nv, piece, 0)[:, None], (piece, cols)
    )

    smem = pl.BlockSpec(memory_space=pltpu.SMEM)
    tiles = 4
    tile = rows // tiles
    ht = tiles // 2

    def whole(shape):
        return pl.BlockSpec(shape, lambda i: (0,) * len(shape))

    row_tile = pl.BlockSpec((tile, cols), lambda i: (i, 0))
    parts = (owners, 2, piece, cols)
    near = pl.pallas_call(
        near_kernel,
        grid=(tiles,),
        in_specs=[smem, row_tile, row_tile],
        out_specs=whole(parts),
        out_shape=jax.ShapeDtypeStruct(parts, BF),
        scratch_shapes=[pltpu.VMEM((2, cols, cols), F32)],
        cost_estimate=pl.CostEstimate(flops=4 * rows * cols * cols, bytes_accessed=4 * rows * cols, transcendentals=0),
        name="near",
    )(sc, own, partner)
    near = lax.all_to_all(near, "grp", 0, 0)
    vm = pl.BlockSpec(memory_space=pltpu.VMEM)
    near, head = pl.pallas_call(
        lambda *refs: near_amplitude_kernel(nv, *refs),
        in_specs=[smem, vm, vm, vm],
        out_specs=[vm, vm],
        out_shape=[jax.ShapeDtypeStruct(parts, BF), jax.ShapeDtypeStruct((16, cols), BF)],
        name="near_amplitude",
    )(sc, near, gaps, vir)
    near = lax.all_to_all(near, "grp", 0, 0)

    low_tile = pl.BlockSpec((tile, cols), lambda i: (i, 0))
    high_tile = pl.BlockSpec((tile, cols), lambda i: (i + ht, 0))
    parts3 = (owners, 3, piece, cols)
    far = pl.pallas_call(
        lambda *refs: far_kernel(half, *refs),
        grid=(ht,),
        in_specs=[smem, low_tile, low_tile, low_tile, high_tile, low_tile, high_tile],
        out_specs=whole(parts3),
        out_shape=jax.ShapeDtypeStruct(parts3, BF),
        scratch_shapes=[pltpu.VMEM((3, cols, cols), F32)],
        cost_estimate=pl.CostEstimate(flops=3 * rows * cols * cols, bytes_accessed=6 * rows * cols, transcendentals=0),
        name="far",
    )(sc, n0, m1, own, own, partner, partner)
    far = lax.all_to_all(far, "grp", 0, 0)
    message = jax.ShapeDtypeStruct((2 * piece + 16, cols), BF)
    sums, up, down, extra = pl.pallas_call(
        pack_kernel,
        in_specs=[vm, vm],
        out_specs=[vm] * 4,
        out_shape=[
            jax.ShapeDtypeStruct((2, piece, cols), F32), message, message,
            jax.ShapeDtypeStruct((piece, cols), BF),
        ],
        name="pack",
    )(far, head)
    below = shift(up, 2)
    above = shift(down, -2)
    extra = swap(extra)
    far = pl.pallas_call(
        lambda *refs: far_amplitude_kernel(nv, *refs),
        in_specs=[smem] + [vm] * 6,
        out_specs=vm,
        out_shape=jax.ShapeDtypeStruct(parts3, BF),
        name="far_amplitude",
    )(sc, sums, above, below, extra, gaps, vir)
    far = lax.all_to_all(far, "grp", 0, 0)

    fifth_block = swap(jnp.where(
        parity == 0, jnp.concatenate([n0, n1], axis=0), jnp.concatenate([m0, m1], axis=0)
    ))
    front = pl.BlockSpec((tile, cols), lambda i: (jnp.minimum(i, ht - 1), 0))
    back = pl.BlockSpec((tile, cols), lambda i: (jnp.maximum(i - ht, 0), 0))
    return pl.pallas_call(
        gamma_kernel,
        grid=(tiles,),
        in_specs=[smem, whole(parts), whole(parts3), row_tile, row_tile, front, back, front, back, row_tile],
        out_specs=row_tile,
        out_shape=jax.ShapeDtypeStruct((rows, cols), three_index.dtype),
        scratch_shapes=[pltpu.VMEM((tile, cols), F32)],
        cost_estimate=pl.CostEstimate(flops=10 * rows * cols * cols, bytes_accessed=14 * rows * cols, transcendentals=0),
        name="gamma",
    )(sc, near, far, own, partner, n0, n1, m0, m1, fifth_block)


def solution(mesh):
    in_specs = (P("grp", "blk"), P("blk"), P(), P(), P())
    out_specs = P("grp", "blk")
    return jax.shard_map(
        per_device, mesh=mesh, in_specs=in_specs, out_specs=out_specs, check_vma=False
    )
```

```python
import jax
import jax.numpy as jnp
from jax import lax
from jax.experimental import pallas as pl
from jax.experimental.pallas import tpu as pltpu
from jax.sharding import PartitionSpec as P


BF = jnp.bfloat16
F32 = jnp.float32
VM = pl.BlockSpec(memory_space=pltpu.VMEM)
SM = pl.BlockSpec(memory_space=pltpu.SMEM)
ANY = pl.BlockSpec(memory_space=pl.ANY)


def mm(a, b):
    return jnp.dot(a, b, preferred_element_type=F32)


def keep_rows(block, start, count):
    row = lax.broadcasted_iota(jnp.int32, block.shape, 0) + start
    return jnp.where(row < count, block, jnp.zeros((), block.dtype))


def fetch(pairs, sems):
    copies = [pltpu.make_async_copy(src, dst, sems.at[j]) for j, (src, dst) in enumerate(pairs)]
    for copy in copies:
        copy.start()
    return copies


def place():
    r = lax.axis_index("blk")
    return r, lax.rem(r, 2), lax.axis_index("grp")


def at(count_ref, index):
    slabs = count_ref.shape[0]
    return count_ref[lax.rem(index + slabs, slabs)]


def three_terms(value):
    hi = value.astype(BF)
    rest = value - hi.astype(F32)
    mid = rest.astype(BF)
    low = (rest - mid.astype(F32)).astype(BF)
    return [hi.astype(F32), mid.astype(F32), low.astype(F32)]


def prep_kernel(
    aux_ref, energy_ref, other_ref, vir_ref, vir_rows_ref, own_ref, p_ref,
    o0t_ref, o1t_ref, pt_ref, near_ref, gaps_ref, head_ref,
):
    _, parity, g = place()
    rows, cols = own_ref.shape
    half = rows // 2
    owners, _, piece, _ = near_ref.shape
    nv = vir_ref.shape[1]
    count = aux_ref[g]
    o0t_ref[...] = keep_rows(own_ref[:half, :], 0, count).T
    o1t_ref[...] = keep_rows(own_ref[half:, :], half, count).T

    @pl.when(parity == 0)
    def _():
        pt_ref[...] = keep_rows(p_ref[:half, :], 0, count).T

    @pl.when(parity == 1)
    def _():
        pt_ref[...] = keep_rows(p_ref[half:, :], half, count).T

    for j, ref in enumerate((own_ref, p_ref)):
        pair = mm(o0t_ref[...], ref[:half, :]) + mm(o1t_ref[...], ref[half:, :])
        near_ref[:, j] = pair.reshape(owners, piece, cols).astype(BF)

    slots = cols // nv
    slot = (g * piece) // nv
    lane = lax.broadcasted_iota(jnp.int32, (1, cols), 1)
    vir = jnp.concatenate([vir_ref[...]] * slots, axis=1)
    rows_out = []
    for ref in (energy_ref, other_ref):
        level = jnp.zeros((1, cols), F32)
        for k in range(slots):
            level = jnp.where(lane // nv == k, ref[k], level)
        rows_out.append(level - vir)
    for ref in (energy_ref, other_ref):
        rows_out.append(jnp.broadcast_to(ref[slot], (1, cols)))
    terms = []
    for row in rows_out:
        terms += three_terms(row)
    zero = jnp.zeros((4, cols), F32)
    head_ref[...] = jnp.concatenate(terms + [zero], axis=0).astype(BF)
    start = pl.multiple_of(lax.rem(g * piece, nv), piece)
    gaps_ref[0:8, :] = jnp.concatenate(rows_out + [zero], axis=0)
    gaps_ref[8:, :] = vir_rows_ref[pl.ds(start, piece), :]


def far_kernel(n_ref, m_ref, o0t_ref, o1t_ref, pt_ref, near_ref, out_ref, n_buf, m_buf, o0_buf, o1_buf, p_buf, sems):
    _, parity, _ = place()
    owners, _, piece, cols = out_ref.shape
    copies = fetch(
        [(n_ref, n_buf), (o0t_ref, o0_buf), (m_ref, m_buf), (o1t_ref, o1_buf), (pt_ref, p_buf)], sems
    )

    def put(j, pair):
        out_ref[:, j] = pair.reshape(owners, piece, cols).astype(BF)

    out_ref[:, 0:2] = near_ref[...]
    copies[0].wait()
    copies[1].wait()
    put(2, mm(o0_buf[...], n_buf[...]).T)
    copies[2].wait()
    copies[3].wait()
    put(3, mm(o1_buf[...], m_buf[...]))
    copies[4].wait()

    @pl.when(parity == 0)
    def _():
        put(4, mm(p_buf[...], n_buf[...]).T)

    @pl.when(parity == 1)
    def _():
        put(4, mm(p_buf[...], m_buf[...]))


def pack_kernel(parts_ref, head_ref, sum_ref, up_ref, down_ref, swap_ref, buf, sems):
    fetch([(parts_ref, buf)], sems)[0].wait()
    total = jnp.sum(buf[...].astype(F32), axis=0)
    sum_ref[...] = total[:4]
    extra = total[4].astype(BF)
    size = extra.shape[0]
    swap_ref[...] = extra
    for j, ref in ((2, up_ref), (3, down_ref)):
        ref[0:size, :] = total[j].astype(BF)
        ref[size:2 * size, :] = extra
        ref[2 * size:, :] = head_ref[...]


def amplitude_kernel(
    nv, count_ref, sum_ref, gaps_ref, above_ref, below_ref, swap_ref, out_ref, above, below, swapped, sems
):
    r, parity, g = place()
    size, cols = swapped.shape
    slot = (g * size) // nv
    copies = fetch([(above_ref, above), (below_ref, below), (swap_ref, swapped)], sems)
    vir = gaps_ref[8:, :]
    own_gap = gaps_ref[0:1, :]
    own_rows = gaps_ref[2:3, :] - vir
    own_count = count_ref[r]
    lane = lax.broadcasted_iota(jnp.int32, (size, cols), 1)

    def put(j, pair, gap_rows, gap_cols, row_count, col_count):
        keep = (lane < col_count * nv) & (slot < row_count)
        amp = jnp.where(keep, pair / (gap_rows + gap_cols), 0.0).astype(BF)
        for owner in range(out_ref.shape[0]):
            out_ref[owner, j] = amp

    put(0, sum_ref[0], own_rows, own_gap, own_count, own_count)
    put(1, sum_ref[1], own_rows, gaps_ref[1:2, :], own_count, count_ref[r + 1 - 2 * parity])
    for copy in copies:
        copy.wait()

    def head(ref, row):
        block = ref[2 * size:, :].astype(F32)
        return block[3 * row:3 * row + 1] + block[3 * row + 1:3 * row + 2] + block[3 * row + 2:3 * row + 3]

    put(
        2, sum_ref[2] + above[0:size, :].astype(F32), head(above, 2) - vir, own_gap,
        at(count_ref, r + 2), own_count,
    )
    put(
        3, sum_ref[3] + below[0:size, :].astype(F32), own_rows, head(below, 0),
        own_count, at(count_ref, r - 2),
    )

    @pl.when(parity == 0)
    def _():
        put(
            4, swapped[...].astype(F32) + below[size:2 * size, :].astype(F32), own_rows, head(below, 1),
            own_count, at(count_ref, r - 1),
        )

    @pl.when(parity == 1)
    def _():
        put(
            4, swapped[...].astype(F32) + above[size:2 * size, :].astype(F32), head(above, 3) - vir, own_gap,
            at(count_ref, r + 1), own_count,
        )


def gamma_kernel(
    aux_ref, amps_ref, o_ref, p_ref, n0_ref, n1_ref, m0_ref, m1_ref, x_ref, out_ref, buf, weights, sems
):
    step = pl.program_id(0)
    tile, cols = o_ref.shape
    _, parity, g = place()

    @pl.when(step == 0)
    def _():
        fetch([(amps_ref, buf)], sems)[0].wait()

        def put(j, turned):
            matrix = buf[:, j].reshape(cols, cols)
            weights[j * cols:(j + 1) * cols, :] = matrix.T if turned else matrix

        put(0, False)
        put(1, True)
        put(2, False)
        put(3, True)

        @pl.when(parity == 0)
        def _():
            put(4, True)

        @pl.when(parity == 1)
        def _():
            put(4, False)

    def finish(n_ref, m_ref):
        blocks = jnp.concatenate([o_ref[...], p_ref[...], n_ref[...], m_ref[...], x_ref[...]], axis=1)
        total = mm(blocks, weights[...])
        out_ref[...] = keep_rows(total, step * tile, aux_ref[g]).astype(out_ref.dtype)

    lower = step < pl.num_programs(0) // 2

    @pl.when(lower)
    def _():
        finish(n0_ref, m0_ref)

    @pl.when(jnp.logical_not(lower))
    def _():
        finish(n1_ref, m1_ref)


def cost(flops, size):
    return pl.CostEstimate(flops=flops, bytes_accessed=size, transcendentals=0)


def per_device(three_index, occ_energy, vir_energy, aux_count, occ_count):
    rows, cols = three_index.shape
    half = rows // 2
    nv = vir_energy.shape[0]
    slabs = lax.axis_size("blk")
    owners = lax.axis_size("grp")
    piece = cols // owners
    dma = pltpu.SemaphoreType.DMA

    def shift(value, steps):
        return lax.ppermute(value, "blk", [(i, (i + steps) % slabs) for i in range(slabs)])

    def swap(value):
        return lax.ppermute(value, "blk", [(i, i ^ 1) for i in range(slabs)])

    def shape(*dims, dtype=BF):
        return jax.ShapeDtypeStruct(dims, dtype)

    own = three_index
    lower, upper = own[:half], own[half:]
    n0 = shift(lower, -2)
    m1 = shift(upper, 2)
    partner = swap(own)
    n1 = shift(upper, -2)
    m0 = shift(lower, 2)
    partner_energy = swap(occ_energy)

    o0t, o1t, pt, near, gaps, head = pl.pallas_call(
        prep_kernel,
        in_specs=[SM, SM, SM, VM, VM, VM, VM],
        out_specs=[VM] * 6,
        out_shape=[
            shape(cols, half), shape(cols, half), shape(cols, half), shape(owners, 2, piece, cols),
            shape(8 + piece, cols, dtype=F32), shape(16, cols),
        ],
        cost_estimate=cost(4 * rows * cols * cols, 8 * rows * cols),
        compiler_params=pltpu.CompilerParams(vmem_limit_bytes=16 << 20),
        name="prep",
    )(
        aux_count, occ_energy, partner_energy, vir_energy[None, :],
        jnp.broadcast_to(vir_energy[:, None], (nv, cols)), own, partner,
    )

    parts = shape(owners, 5, piece, cols)
    partial_sums = pl.pallas_call(
        far_kernel,
        in_specs=[ANY] * 5 + [VM],
        out_specs=VM,
        out_shape=parts,
        scratch_shapes=[
            pltpu.VMEM((half, cols), BF), pltpu.VMEM((half, cols), BF), pltpu.VMEM((cols, half), BF),
            pltpu.VMEM((cols, half), BF), pltpu.VMEM((cols, half), BF), dma((5,)),
        ],
        cost_estimate=cost(3 * rows * cols * cols, 5 * rows * cols),
        compiler_params=pltpu.CompilerParams(vmem_limit_bytes=10 << 20),
        name="far",
    )(n0, m1, o0t, o1t, pt, near)
    pieces = lax.all_to_all(partial_sums, "grp", 0, 0)
    message = shape(2 * piece + 16, cols)
    sums, up, down, extra = pl.pallas_call(
        pack_kernel,
        in_specs=[ANY, VM],
        out_specs=[VM] * 4,
        out_shape=[shape(4, piece, cols, dtype=F32), message, message, shape(piece, cols)],
        scratch_shapes=[pltpu.VMEM(parts.shape, BF), dma((1,))],
        cost_estimate=cost(cols * cols, 4 * cols * cols),
        compiler_params=pltpu.CompilerParams(vmem_limit_bytes=6 << 20),
        name="pack",
    )(pieces, head)
    below = shift(up, 2)
    above = shift(down, -2)
    extra = swap(extra)
    amps = pl.pallas_call(
        lambda *refs: amplitude_kernel(nv, *refs),
        in_specs=[SM, VM, VM, ANY, ANY, ANY],
        out_specs=VM,
        out_shape=parts,
        scratch_shapes=[
            pltpu.VMEM(message.shape, BF), pltpu.VMEM(message.shape, BF), pltpu.VMEM((piece, cols), BF), dma((3,)),
        ],
        cost_estimate=cost(cols * cols, 8 * cols * cols),
        compiler_params=pltpu.CompilerParams(vmem_limit_bytes=6 << 20),
        name="amplitude",
    )(occ_count, sums, gaps, above, below, extra)
    amps = lax.all_to_all(amps, "grp", 0, 0)

    parity = lax.axis_index("blk") % 2
    fifth = swap(jnp.where(
        parity == 0, jnp.concatenate([n0, n1], axis=0), jnp.concatenate([m0, m1], axis=0)
    ))

    tiles = 4
    tile = rows // tiles
    ht = tiles // 2
    row_tile = pl.BlockSpec((tile, cols), lambda i: (i, 0))
    front = pl.BlockSpec((tile, cols), lambda i: (jnp.minimum(i, ht - 1), 0))
    back = pl.BlockSpec((tile, cols), lambda i: (jnp.maximum(i - ht, 0), 0))
    return pl.pallas_call(
        gamma_kernel,
        grid=(tiles,),
        in_specs=[SM, ANY, row_tile, row_tile, front, back, front, back, row_tile],
        out_specs=row_tile,
        out_shape=jax.ShapeDtypeStruct((rows, cols), three_index.dtype),
        scratch_shapes=[pltpu.VMEM(parts.shape, BF), pltpu.VMEM((5 * cols, cols), BF), dma((1,))],
        cost_estimate=cost(10 * rows * cols * cols, 14 * rows * cols),
        compiler_params=pltpu.CompilerParams(vmem_limit_bytes=16 << 20),
        name="gamma",
    )(aux_count, amps, own, partner, n0, n1, m0, m1, fifth)


def solution(mesh):
    in_specs = (P("grp", "blk"), P("blk"), P(), P(), P())
    out_specs = P("grp", "blk")
    return jax.shard_map(
        per_device, mesh=mesh, in_specs=in_specs, out_specs=out_specs, check_vma=False
    )
```

```python
import jax
import jax.numpy as jnp
from jax import lax
from jax.experimental import pallas as pl
from jax.experimental.pallas import tpu as pltpu
from jax.sharding import Mesh, PartitionSpec as P


BF = jnp.bfloat16
F32 = jnp.float32
VM = pl.BlockSpec(memory_space=pltpu.VMEM)
SM = pl.BlockSpec(memory_space=pltpu.SMEM)
ANY = pl.BlockSpec(memory_space=pl.ANY)


def mm(a, b):
    return jnp.dot(a, b, preferred_element_type=F32)


def keep_rows(block, start, count):
    row = lax.broadcasted_iota(jnp.int32, block.shape, 0) + start
    return jnp.where(row < count, block, jnp.zeros((), block.dtype))


def place():
    return lax.axis_index("ch"), lax.axis_index("core"), lax.axis_index("grp")


def piece_start(piece):
    return (lax.axis_index("core") * lax.axis_size("grp") + lax.axis_index("grp")) * piece


def at(count_ref, index):
    slabs = count_ref.shape[0]
    return count_ref[lax.rem(index + slabs, slabs)]


def three_terms(value):
    hi = value.astype(BF)
    rest = value - hi.astype(F32)
    mid = rest.astype(BF)
    low = (rest - mid.astype(F32)).astype(BF)
    return [hi.astype(F32), mid.astype(F32), low.astype(F32)]


def prep_kernel(
    aux_ref, energy_ref, other_ref, vir_ref, vir_rows_ref, own_ref, p_ref,
    o0t_ref, o1t_ref, pt_ref, near_ref, gaps_ref, head_ref,
):
    _, parity, g = place()
    rows, cols = own_ref.shape
    half = rows // 2
    members, _, piece, _ = near_ref.shape
    nv = vir_ref.shape[1]
    count = aux_ref[g]
    o0t_ref[...] = keep_rows(own_ref[:half, :], 0, count).T
    o1t_ref[...] = keep_rows(own_ref[half:, :], half, count).T

    def put(j, pair):
        near_ref[:, j] = pair.reshape(members, piece, cols).astype(BF)

    put(0, mm(o0t_ref[...], own_ref[:half, :]) + mm(o1t_ref[...], own_ref[half:, :]))

    @pl.when(parity == 0)
    def _():
        pt_ref[...] = keep_rows(p_ref[:half, :], 0, count).T
        put(1, mm(o0t_ref[...], p_ref[:half, :]))

    @pl.when(parity == 1)
    def _():
        pt_ref[...] = keep_rows(p_ref[half:, :], half, count).T
        put(1, mm(pt_ref[...], own_ref[half:, :]))

    slots = cols // nv
    first_row = piece_start(piece)
    slot = first_row // nv
    lane = lax.broadcasted_iota(jnp.int32, (1, cols), 1)
    vir = jnp.concatenate([vir_ref[...]] * slots, axis=1)
    even = parity == 0
    levels = [
        [jnp.where(even, energy_ref[k], other_ref[k]) for k in range(slots)],
        [jnp.where(even, other_ref[k], energy_ref[k]) for k in range(slots)],
    ]
    rows_out = []
    for level_of in levels:
        level = jnp.zeros((1, cols), F32)
        for k in range(slots):
            level = jnp.where(lane // nv == k, level_of[k], level)
        rows_out.append(level - vir)
    for level_of in levels:
        level = jnp.zeros((1, cols), F32)
        for k in range(slots):
            level = jnp.where(slot == k, level_of[k], level)
        rows_out.append(level)
    terms = []
    for row in rows_out:
        terms += three_terms(row)
    zero = jnp.zeros((4, cols), F32)
    head_ref[...] = jnp.concatenate(terms + [zero], axis=0).astype(BF)
    start = pl.multiple_of(lax.rem(first_row, nv), piece)
    gaps_ref[0:8, :] = jnp.concatenate(rows_out + [zero], axis=0)
    gaps_ref[8:, :] = vir_rows_ref[pl.ds(start, piece), :]


def far_kernel(n_ref, m_ref, o0t_ref, o1t_ref, pt_ref, near_ref, out_ref):
    _, parity, _ = place()
    members, _, piece, cols = out_ref.shape

    def put(j, pair):
        out_ref[:, j] = pair.reshape(members, piece, cols).astype(BF)

    out_ref[:, 0:2] = near_ref[...]
    put(2, mm(o0t_ref[...], n_ref[...]).T)
    put(3, mm(o1t_ref[...], m_ref[...]))

    @pl.when(parity == 0)
    def _():
        put(4, mm(pt_ref[...], n_ref[...]).T)

    @pl.when(parity == 1)
    def _():
        put(4, mm(pt_ref[...], m_ref[...]))


def pack_kernel(parts_ref, head_ref, sum_ref, up_ref, down_ref):
    members = parts_ref.shape[0]
    even = jnp.sum(parts_ref[:members // 2].astype(F32), axis=0)
    odd = jnp.sum(parts_ref[members // 2:].astype(F32), axis=0)
    size = head_ref.shape[0]
    pairs = [
        even[0], odd[0], even[1] + odd[1], even[2], odd[2], even[4], even[3], odd[3], odd[4],
    ]
    for j, pair in enumerate(pairs):
        sum_ref[j] = pair
    for first_pair, ref in ((3, up_ref), (6, down_ref)):
        for j in range(3):
            ref[j * size:(j + 1) * size, :] = pairs[first_pair + j].astype(BF)
        ref[3 * size:, :] = head_ref[...]


def amplitude_kernel(nv, count_ref, sum_ref, gaps_ref, above_ref, below_ref, out_ref):
    chip, _, _ = place()
    members, _, size, cols = out_ref.shape
    slot = piece_start(size) // nv
    vir = gaps_ref[8:, :]
    lane = lax.broadcasted_iota(jnp.int32, (size, cols), 1)

    def heads(ref):
        block = ref[3 * size:, :].astype(F32)
        return [block[3 * j:3 * j + 1] + block[3 * j + 1:3 * j + 2] + block[3 * j + 2:3 * j + 3] for j in range(4)]

    def slab_pair(gaps, position):
        counts = [at(count_ref, 2 * position + j) for j in range(2)]
        return [(gaps[j], gaps[2 + j] - vir, counts[j]) for j in range(2)]

    here = slab_pair([gaps_ref[j:j + 1, :] for j in range(4)], chip)
    upper = slab_pair(heads(above_ref), chip + 1)
    lower = slab_pair(heads(below_ref), chip - 1)

    def amp(pair, row_slab, col_slab):
        keep = (lane < col_slab[2] * nv) & (slot < row_slab[2])
        return jnp.where(keep, pair / (row_slab[1] + col_slab[0]), 0.0).astype(BF)

    def send(core, j, value):
        for member in range(core * members // 2, (core + 1) * members // 2):
            out_ref[member, j] = value

    def other(ref, j):
        return ref[j * size:(j + 1) * size, :].astype(F32)

    for core in range(2):
        send(core, 0, amp(sum_ref[core], here[core], here[core]))
        send(core, 2, amp(sum_ref[3 + core] + other(above_ref, core), upper[core], here[core]))
        send(core, 3, amp(sum_ref[6 + core] + other(below_ref, core), here[core], lower[core]))
    both = amp(sum_ref[2], here[0], here[1])
    send(0, 1, both)
    send(1, 1, both)
    send(0, 4, amp(sum_ref[8] + other(below_ref, 2), here[0], lower[1]))
    send(1, 4, amp(sum_ref[5] + other(above_ref, 2), upper[0], here[1]))


def gamma_kernel(
    aux_ref, amps_ref, o_ref, p_ref, n0_ref, n1_ref, m0_ref, m1_ref, x_ref, out_ref, result, weights, sems
):
    rows, cols = o_ref.shape
    half = rows // 2
    _, parity, g = place()

    def put(j, turned):
        matrix = amps_ref[:, j].reshape(cols, cols)
        weights[j * cols:(j + 1) * cols, :] = matrix.T if turned else matrix

    put(0, False)
    put(2, False)
    put(3, True)

    @pl.when(parity == 0)
    def _():
        put(1, True)
        put(4, True)

    @pl.when(parity == 1)
    def _():
        put(1, False)
        put(4, False)

    tile = rows // sems.shape[0]
    copies = []
    for j in range(sems.shape[0]):
        start = j * tile
        n_ref, m_ref, low = (n0_ref, m0_ref, start) if start < half else (n1_ref, m1_ref, start - half)
        here, there = pl.ds(start, tile), pl.ds(low, tile)
        blocks = jnp.concatenate(
            [o_ref[here, :], p_ref[here, :], n_ref[there, :], m_ref[there, :], x_ref[here, :]], axis=1
        )
        result[here, :] = keep_rows(mm(blocks, weights[...]), start, aux_ref[g]).astype(result.dtype)
        copy = pltpu.make_async_copy(result.at[here, :], out_ref.at[here, :], sems.at[j])
        copy.start()
        copies.append(copy)
    for copy in copies:
        copy.wait()


def cost(flops, size):
    return pl.CostEstimate(flops=flops, bytes_accessed=size, transcendentals=0)


def memory(mebibytes):
    return pltpu.CompilerParams(vmem_limit_bytes=mebibytes << 20)


def per_device(three_index, occ_energy, vir_energy, aux_count, occ_count):
    rows, cols = three_index.shape
    half = rows // 2
    nv = vir_energy.shape[0]
    chips = lax.axis_size("ch")
    members = 2 * lax.axis_size("grp")
    piece = cols // members

    def shift(value, steps):
        return lax.ppermute(value, "ch", [(i, (i + steps) % chips) for i in range(chips)])

    def swap(value):
        return lax.ppermute(value, "core", [(0, 1), (1, 0)])

    def exchange(value):
        return lax.all_to_all(value, ("core", "grp"), 0, 0)

    def shape(*dims, dtype=BF):
        return jax.ShapeDtypeStruct(dims, dtype)

    own = three_index
    lower, upper = own[:half], own[half:]
    n0 = shift(lower, -1)
    m1 = shift(upper, 1)
    partner = swap(own)
    n1 = shift(upper, -1)
    m0 = shift(lower, 1)
    partner_energy = swap(occ_energy)

    o0t, o1t, pt, near, gaps, head = pl.pallas_call(
        prep_kernel,
        in_specs=[SM, SM, SM, VM, VM, VM, VM],
        out_specs=[VM] * 6,
        out_shape=[
            shape(cols, half), shape(cols, half), shape(cols, half), shape(members, 2, piece, cols),
            shape(8 + piece, cols, dtype=F32), shape(16, cols),
        ],
        cost_estimate=cost(3 * rows * cols * cols, 8 * rows * cols),
        compiler_params=memory(16),
        name="prep",
    )(
        aux_count, occ_energy, partner_energy, vir_energy[None, :],
        jnp.broadcast_to(vir_energy[:, None], (nv, cols)), own, partner,
    )

    parts = shape(members, 5, piece, cols)
    partial_sums = pl.pallas_call(
        far_kernel,
        in_specs=[VM] * 6,
        out_specs=VM,
        out_shape=parts,
        cost_estimate=cost(3 * rows * cols * cols, 5 * rows * cols),
        compiler_params=memory(12),
        name="far",
    )(n0, m1, o0t, o1t, pt, near)
    pieces = exchange(partial_sums)
    message = shape(3 * piece + 16, cols)
    sums, up, down = pl.pallas_call(
        pack_kernel,
        in_specs=[VM, VM],
        out_specs=[VM] * 3,
        out_shape=[shape(9, piece, cols, dtype=F32), message, message],
        cost_estimate=cost(cols * cols, 4 * cols * cols),
        compiler_params=memory(6),
        name="pack",
    )(pieces, head)
    below = shift(up, 1)
    above = shift(down, -1)
    amps = pl.pallas_call(
        lambda *refs: amplitude_kernel(nv, *refs),
        in_specs=[SM] + [VM] * 4,
        out_specs=VM,
        out_shape=parts,
        cost_estimate=cost(cols * cols, 8 * cols * cols),
        compiler_params=memory(6),
        name="amplitude",
    )(occ_count, sums, gaps, above, below)
    amps = exchange(amps)
    fifth = swap(jnp.where(
        lax.axis_index("core") == 0, jnp.concatenate([n0, n1], axis=0), jnp.concatenate([m0, m1], axis=0)
    ))

    tiles = 8
    return pl.pallas_call(
        gamma_kernel,
        in_specs=[SM] + [VM] * 8,
        out_specs=ANY,
        out_shape=jax.ShapeDtypeStruct((rows, cols), three_index.dtype),
        scratch_shapes=[
            pltpu.VMEM((rows, cols), three_index.dtype), pltpu.VMEM((5 * cols, cols), BF),
            pltpu.SemaphoreType.DMA((tiles,)),
        ],
        cost_estimate=cost(10 * rows * cols * cols, 14 * rows * cols),
        compiler_params=memory(20),
        name="gamma",
    )(aux_count, amps, own, partner, n0, n1, m0, m1, fifth)


def solution(mesh):
    chips = mesh.shape["blk"] // 2
    cores = Mesh(mesh.devices.reshape(chips, 2, mesh.shape["grp"]), ("ch", "core", "grp"))
    blocks = P("grp", ("ch", "core"))
    return jax.shard_map(
        per_device, mesh=cores, in_specs=(blocks, P(("ch", "core")), P(), P(), P()), out_specs=blocks,
        check_vma=False,
    )
```

```python
import jax
import jax.numpy as jnp
from jax import lax
from jax.experimental import pallas as pl
from jax.experimental.pallas import tpu as pltpu
from jax.sharding import PartitionSpec as P


BF = jnp.bfloat16
F32 = jnp.float32
VM = pl.BlockSpec(memory_space=pltpu.VMEM)
SM = pl.BlockSpec(memory_space=pltpu.SMEM)
ANY = pl.BlockSpec(memory_space=pl.ANY)


def mm(a, b):
    return jnp.dot(a, b, preferred_element_type=F32)


def keep_rows(block, start, count):
    row = lax.broadcasted_iota(jnp.int32, block.shape, 0) + start
    return jnp.where(row < count, block, jnp.zeros((), block.dtype))


def place():
    r = lax.axis_index("blk")
    return r, lax.rem(r, 2), lax.axis_index("grp")


def at(count_ref, index):
    slabs = count_ref.shape[0]
    return count_ref[lax.rem(index + slabs, slabs)]


def halves_kernel(own_ref, lower_ref, upper_ref, sems):
    half = lower_ref.shape[0]
    copies = [
        pltpu.make_async_copy(own_ref.at[j * half:(j + 1) * half], ref, sems.at[j])
        for j, ref in enumerate((lower_ref, upper_ref))
    ]
    for copy in copies:
        copy.start()
    for copy in copies:
        copy.wait()


def three_terms(value):
    hi = value.astype(BF)
    rest = value - hi.astype(F32)
    mid = rest.astype(BF)
    low = (rest - mid.astype(F32)).astype(BF)
    return [hi.astype(F32), mid.astype(F32), low.astype(F32)]


def prep_kernel(
    aux_ref, energy_ref, other_ref, vir_ref, vir_rows_ref, own_ref, p_ref,
    o0t_ref, o1t_ref, pt_ref, near_ref, gaps_ref, head_ref,
):
    _, parity, g = place()
    rows, cols = own_ref.shape
    half = rows // 2
    owners, _, piece, _ = near_ref.shape
    nv = vir_ref.shape[1]
    count = aux_ref[g]
    o0t_ref[...] = keep_rows(own_ref[:half, :], 0, count).T
    o1t_ref[...] = keep_rows(own_ref[half:, :], half, count).T

    @pl.when(parity == 0)
    def _():
        pt_ref[...] = keep_rows(p_ref[:half, :], 0, count).T

    @pl.when(parity == 1)
    def _():
        pt_ref[...] = keep_rows(p_ref[half:, :], half, count).T

    for j, ref in enumerate((own_ref, p_ref)):
        pair = mm(o0t_ref[...], ref[:half, :]) + mm(o1t_ref[...], ref[half:, :])
        near_ref[:, j] = pair.reshape(owners, piece, cols).astype(BF)

    slots = cols // nv
    slot = (g * piece) // nv
    lane = lax.broadcasted_iota(jnp.int32, (1, cols), 1)
    vir = jnp.concatenate([vir_ref[...]] * slots, axis=1)
    rows_out = []
    for ref in (energy_ref, other_ref):
        level = jnp.zeros((1, cols), F32)
        for k in range(slots):
            level = jnp.where(lane // nv == k, ref[k], level)
        rows_out.append(level - vir)
    for ref in (energy_ref, other_ref):
        rows_out.append(jnp.broadcast_to(ref[slot], (1, cols)))
    terms = []
    for row in rows_out:
        terms += three_terms(row)
    zero = jnp.zeros((4, cols), F32)
    head_ref[...] = jnp.concatenate(terms + [zero], axis=0).astype(BF)
    start = pl.multiple_of(lax.rem(g * piece, nv), piece)
    gaps_ref[0:8, :] = jnp.concatenate(rows_out + [zero], axis=0)
    gaps_ref[8:, :] = vir_rows_ref[pl.ds(start, piece), :]


def far_kernel(n_ref, m_ref, o0t_ref, o1t_ref, pt_ref, out_ref):
    _, parity, _ = place()
    owners, _, piece, cols = out_ref.shape

    def put(j, pair):
        out_ref[:, j] = pair.reshape(owners, piece, cols).astype(BF)

    put(0, mm(o0t_ref[...], n_ref[...]).T)
    put(1, mm(o1t_ref[...], m_ref[...]))

    @pl.when(parity == 0)
    def _():
        put(2, mm(pt_ref[...], n_ref[...]).T)

    @pl.when(parity == 1)
    def _():
        put(2, mm(pt_ref[...], m_ref[...]))


def pack_kernel(parts_ref, head_ref, sum_ref, up_ref, down_ref, swap_ref):
    total = jnp.sum(parts_ref[...].astype(F32), axis=0)
    sum_ref[...] = total[:2]
    extra = total[2].astype(BF)
    size = extra.shape[0]
    swap_ref[...] = extra
    for j, ref in ((0, up_ref), (1, down_ref)):
        ref[0:size, :] = total[j].astype(BF)
        ref[size:2 * size, :] = extra
        ref[2 * size:, :] = head_ref[...]


def amplitude_kernel(nv, count_ref, near_ref, sum_ref, gaps_ref, above_ref, below_ref, swap_ref, out_ref):
    r, parity, g = place()
    size, cols = swap_ref.shape
    slot = (g * size) // nv
    vir = gaps_ref[8:, :]
    own_gap = gaps_ref[0:1, :]
    own_rows = gaps_ref[2:3, :] - vir
    own_count = count_ref[r]
    lane = lax.broadcasted_iota(jnp.int32, (size, cols), 1)

    def put(j, pair, gap_rows, gap_cols, row_count, col_count):
        keep = (lane < col_count * nv) & (slot < row_count)
        amp = jnp.where(keep, pair / (gap_rows + gap_cols), 0.0).astype(BF)
        for owner in range(out_ref.shape[0]):
            out_ref[owner, j] = amp

    def head(ref, row):
        block = ref[2 * size:, :].astype(F32)
        return block[3 * row:3 * row + 1] + block[3 * row + 1:3 * row + 2] + block[3 * row + 2:3 * row + 3]

    near = jnp.sum(near_ref[...].astype(F32), axis=0)
    put(0, near[0], own_rows, own_gap, own_count, own_count)
    put(1, near[1], own_rows, gaps_ref[1:2, :], own_count, count_ref[r + 1 - 2 * parity])
    put(
        2, sum_ref[0] + above_ref[0:size, :].astype(F32), head(above_ref, 2) - vir, own_gap,
        at(count_ref, r + 2), own_count,
    )
    put(
        3, sum_ref[1] + below_ref[0:size, :].astype(F32), own_rows, head(below_ref, 0),
        own_count, at(count_ref, r - 2),
    )
    other = swap_ref[...].astype(F32)

    @pl.when(parity == 0)
    def _():
        put(
            4, other + below_ref[size:2 * size, :].astype(F32), own_rows, head(below_ref, 1),
            own_count, at(count_ref, r - 1),
        )

    @pl.when(parity == 1)
    def _():
        put(
            4, other + above_ref[size:2 * size, :].astype(F32), head(above_ref, 3) - vir, own_gap,
            at(count_ref, r + 1), own_count,
        )


def gamma_kernel(
    aux_ref, amps_ref, o_ref, p_ref, n0_ref, n1_ref, m0_ref, m1_ref, x_ref, out_ref,
    p_buf, n_buf, m_buf, result, weights, sems,
):
    rows, cols = o_ref.shape
    half = rows // 2
    _, parity, g = place()
    tiles = sems.shape[1]
    tile = rows // tiles
    starts = [j * tile for j in range(tiles)]
    fetches = {}
    for j, start in enumerate(starts):
        here = pl.ds(start, tile)
        wanted = [(p_ref.at[here, :], p_buf.at[here, :])]
        if start < half:
            wanted.append((m0_ref.at[here, :], m_buf.at[here, :]))
        else:
            low = pl.ds(start - half, tile)
            wanted.append((n1_ref.at[low, :], n_buf.at[low, :]))
        fetches[j] = [pltpu.make_async_copy(src, dst, sems.at[k, j]) for k, (src, dst) in enumerate(wanted)]
        for copy in fetches[j]:
            copy.start()

    def put(j, turned):
        matrix = amps_ref[:, j].reshape(cols, cols)
        weights[j * cols:(j + 1) * cols, :] = matrix.T if turned else matrix

    put(0, False)
    put(1, True)
    put(2, False)
    put(3, True)

    @pl.when(parity == 0)
    def _():
        put(4, True)

    @pl.when(parity == 1)
    def _():
        put(4, False)

    copies = []
    for j, start in enumerate(starts):
        n_ref, m_ref, low = (n0_ref, m_buf, start) if start < half else (n_buf, m1_ref, start - half)
        here, there = pl.ds(start, tile), pl.ds(low, tile)
        for copy in fetches[j]:
            copy.wait()
        blocks = jnp.concatenate(
            [o_ref[here, :], p_buf[here, :], n_ref[there, :], m_ref[there, :], x_ref[here, :]], axis=1
        )
        result[here, :] = keep_rows(mm(blocks, weights[...]), start, aux_ref[g]).astype(result.dtype)
        copy = pltpu.make_async_copy(result.at[here, :], out_ref.at[here, :], sems.at[2, j])
        copy.start()
        copies.append(copy)
    for copy in copies:
        copy.wait()


def cost(flops, size):
    return pl.CostEstimate(flops=flops, bytes_accessed=size, transcendentals=0)


def memory(mebibytes):
    return pltpu.CompilerParams(vmem_limit_bytes=mebibytes << 20)


def per_device(three_index, occ_energy, vir_energy, aux_count, occ_count):
    rows, cols = three_index.shape
    half = rows // 2
    nv = vir_energy.shape[0]
    slabs = lax.axis_size("blk")
    owners = lax.axis_size("grp")
    piece = cols // owners
    dma = pltpu.SemaphoreType.DMA

    def shift(value, steps):
        return lax.ppermute(value, "blk", [(i, (i + steps) % slabs) for i in range(slabs)])

    def swap(value):
        return lax.ppermute(value, "blk", [(i, i ^ 1) for i in range(slabs)])

    def shape(*dims, dtype=BF):
        return jax.ShapeDtypeStruct(dims, dtype)

    own = three_index
    lower, upper = pl.pallas_call(
        halves_kernel,
        in_specs=[ANY],
        out_specs=[VM, VM],
        out_shape=[shape(half, cols), shape(half, cols)],
        scratch_shapes=[dma((2,))],
        cost_estimate=cost(0, 4 * rows * cols),
        compiler_params=memory(8),
        name="halves",
    )(own)
    n0 = shift(lower, -2)
    m1 = shift(upper, 2)
    partner = swap(own)
    partner_energy = swap(occ_energy)

    o0t, o1t, pt, near, gaps, head = pl.pallas_call(
        prep_kernel,
        in_specs=[SM, SM, SM, VM, VM, VM, VM],
        out_specs=[VM] * 6,
        out_shape=[
            shape(cols, half), shape(cols, half), shape(cols, half), shape(owners, 2, piece, cols),
            shape(8 + piece, cols, dtype=F32), shape(16, cols),
        ],
        cost_estimate=cost(4 * rows * cols * cols, 8 * rows * cols),
        compiler_params=memory(16),
        name="prep",
    )(
        aux_count, occ_energy, partner_energy, vir_energy[None, :],
        jnp.broadcast_to(vir_energy[:, None], (nv, cols)), own, partner,
    )
    upper, lower, near = lax.optimization_barrier((upper, lower, near))
    n1 = shift(upper, -2)
    m0 = shift(lower, 2)
    near = lax.all_to_all(near, "grp", 0, 0)
    n0, m1, near = lax.optimization_barrier((n0, m1, near))
    parts = shape(owners, 3, piece, cols)
    partial_sums = pl.pallas_call(
        far_kernel,
        in_specs=[VM] * 5,
        out_specs=VM,
        out_shape=parts,
        cost_estimate=cost(3 * rows * cols * cols, 5 * rows * cols),
        compiler_params=memory(12),
        name="far",
    )(n0, m1, o0t, o1t, pt)
    pieces = lax.all_to_all(partial_sums, "grp", 0, 0)
    message = shape(2 * piece + 16, cols)
    sums, up, down, extra = pl.pallas_call(
        pack_kernel,
        in_specs=[VM, VM],
        out_specs=[VM] * 4,
        out_shape=[shape(2, piece, cols, dtype=F32), message, message, shape(piece, cols)],
        cost_estimate=cost(cols * cols, 4 * cols * cols),
        compiler_params=memory(6),
        name="pack",
    )(pieces, head)
    below = shift(up, 2)
    above = shift(down, -2)
    extra = swap(extra)
    amps = pl.pallas_call(
        lambda *refs: amplitude_kernel(nv, *refs),
        in_specs=[SM] + [VM] * 6,
        out_specs=VM,
        out_shape=shape(owners, 5, piece, cols),
        cost_estimate=cost(cols * cols, 8 * cols * cols),
        compiler_params=memory(6),
        name="amplitude",
    )(occ_count, near, sums, gaps, above, below, extra)
    amps = lax.all_to_all(amps, "grp", 0, 0)
    fifth = swap(jnp.where(
        lax.axis_index("blk") % 2 == 0, jnp.concatenate([n0, n1], axis=0), jnp.concatenate([m0, m1], axis=0)
    ))

    tiles = 4
    return pl.pallas_call(
        gamma_kernel,
        in_specs=[SM, VM, VM, ANY, VM, ANY, ANY, VM, VM],
        out_specs=ANY,
        out_shape=jax.ShapeDtypeStruct((rows, cols), three_index.dtype),
        scratch_shapes=[
            pltpu.VMEM((rows, cols), BF), pltpu.VMEM((half, cols), BF), pltpu.VMEM((half, cols), BF),
            pltpu.VMEM((rows, cols), three_index.dtype), pltpu.VMEM((5 * cols, cols), BF), dma((3, tiles)),
        ],
        cost_estimate=cost(10 * rows * cols * cols, 14 * rows * cols),
        compiler_params=memory(20),
        name="gamma",
    )(aux_count, amps, own, partner, n0, n1, m0, m1, fifth)


def solution(mesh):
    in_specs = (P("grp", "blk"), P("blk"), P(), P(), P())
    out_specs = P("grp", "blk")
    return jax.shard_map(
        per_device, mesh=mesh, in_specs=in_specs, out_specs=out_specs, check_vma=False
    )
```

```python
import jax
import jax.numpy as jnp
from jax import lax
from jax.experimental import pallas as pl
from jax.experimental.pallas import tpu as pltpu
from jax.sharding import PartitionSpec as P


BF = jnp.bfloat16
F32 = jnp.float32
VM = pl.BlockSpec(memory_space=pltpu.VMEM)
SM = pl.BlockSpec(memory_space=pltpu.SMEM)
ANY = pl.BlockSpec(memory_space=pl.ANY)


def mm(a, b):
    return jnp.dot(a, b, preferred_element_type=F32)


def keep_rows(block, start, count):
    row = lax.broadcasted_iota(jnp.int32, block.shape, 0) + start
    return jnp.where(row < count, block, jnp.zeros((), block.dtype))


def place():
    r = lax.axis_index("blk")
    return r, lax.rem(r, 2), lax.axis_index("grp")


def at(count_ref, index):
    slabs = count_ref.shape[0]
    return count_ref[lax.rem(index + slabs, slabs)]


def three_terms(value):
    hi = value.astype(BF)
    rest = value - hi.astype(F32)
    mid = rest.astype(BF)
    low = (rest - mid.astype(F32)).astype(BF)
    return [hi.astype(F32), mid.astype(F32), low.astype(F32)]


def prep_kernel(
    aux_ref, energy_ref, other_ref, vir_ref, vir_rows_ref, own_ref, p_ref,
    o0t_ref, o1t_ref, pt_ref, near_ref, gaps_ref, head_ref,
):
    _, parity, g = place()
    rows, cols = own_ref.shape
    half = rows // 2
    owners = near_ref.shape[0]
    piece = cols // owners
    part = piece // 2
    nv = vir_ref.shape[1]
    count = aux_ref[g]
    o0t_ref[...] = keep_rows(own_ref[:half, :], 0, count).T
    o1t_ref[...] = keep_rows(own_ref[half:, :], half, count).T

    @pl.when(parity == 0)
    def _():
        pt_ref[...] = keep_rows(p_ref[:half, :], 0, count).T

    @pl.when(parity == 1)
    def _():
        pt_ref[...] = keep_rows(p_ref[half:, :], half, count).T

    def put(rows_of, pair):
        near_ref[:, rows_of] = pair.reshape(owners, pair.shape[0] // owners, cols).astype(BF)

    put(slice(0, piece), mm(o0t_ref[...], own_ref[:half, :]) + mm(o1t_ref[...], own_ref[half:, :]))
    middle = cols // 2

    @pl.when(parity == 0)
    def _():
        put(
            slice(piece, piece + part),
            mm(o0t_ref[:middle, :], p_ref[:half, :]) + mm(o1t_ref[:middle, :], p_ref[half:, :]),
        )

    @pl.when(parity == 1)
    def _():
        low = keep_rows(p_ref[:half, middle:], 0, count).T
        put(
            slice(piece, piece + part),
            mm(low, own_ref[:half, :]) + mm(pt_ref[middle:, :], own_ref[half:, :]),
        )

    slots = cols // nv
    slot = (g * piece) // nv
    lane = lax.broadcasted_iota(jnp.int32, (1, cols), 1)
    vir = jnp.concatenate([vir_ref[...]] * slots, axis=1)
    rows_out = []
    for ref in (energy_ref, other_ref):
        level = jnp.zeros((1, cols), F32)
        for k in range(slots):
            level = jnp.where(lane // nv == k, ref[k], level)
        rows_out.append(level - vir)
    for ref in (energy_ref, other_ref):
        rows_out.append(jnp.broadcast_to(ref[slot], (1, cols)))
    terms = []
    for row in rows_out:
        terms += three_terms(row)
    zero = jnp.zeros((4, cols), F32)
    head_ref[...] = jnp.concatenate(terms + [zero], axis=0).astype(BF)
    for upper_half in range(2):
        k = (g * part) // nv + upper_half * (slots // 2)
        level = jnp.where(parity == 0, energy_ref[k], other_ref[k])
        rows_out.append(jnp.broadcast_to(level, (1, cols)))
    gaps_ref[0:8, :] = jnp.concatenate(rows_out + [zero[:2]], axis=0)
    start = pl.multiple_of(lax.rem(g * piece, nv), piece)
    gaps_ref[8:8 + piece, :] = vir_rows_ref[pl.ds(start, piece), :]
    start = pl.multiple_of(lax.rem(g * part, nv), part)
    gaps_ref[8 + piece:, :] = vir_rows_ref[pl.ds(start, part), :]


def far_kernel(n_ref, m_ref, o0t_ref, o1t_ref, pt_ref, near_ref, out_ref):
    _, parity, _ = place()
    owners, _, cols = out_ref.shape
    piece = cols // owners
    near = near_ref.shape[1]

    def put(j, pair):
        out_ref[:, near + j * piece:near + (j + 1) * piece] = pair.reshape(owners, piece, cols).astype(BF)

    out_ref[:, 0:near] = near_ref[...]
    put(0, mm(o0t_ref[...], n_ref[...]).T)
    put(1, mm(o1t_ref[...], m_ref[...]))

    @pl.when(parity == 0)
    def _():
        put(2, mm(pt_ref[...], n_ref[...]).T)

    @pl.when(parity == 1)
    def _():
        put(2, mm(pt_ref[...], m_ref[...]))


def pack_kernel(parts_ref, head_ref, sum_ref, up_ref, down_ref, swap_ref):
    total = jnp.sum(parts_ref[...].astype(F32), axis=0)
    size = parts_ref.shape[2] // parts_ref.shape[0]
    part = size // 2
    near = size + part
    sum_ref[0:size, :] = total[0:size]
    sum_ref[size:3 * size, :] = total[near:near + 2 * size]
    sum_ref[3 * size:, :] = total[size:near]
    extra = total[near + 2 * size:].astype(BF)
    swap_ref[0:size, :] = extra
    swap_ref[size:, :] = total[size:near].astype(BF)
    for j, ref in ((0, up_ref), (1, down_ref)):
        ref[0:size, :] = total[near + j * size:near + (j + 1) * size].astype(BF)
        ref[size:2 * size, :] = extra
        ref[2 * size:, :] = head_ref[...]


def amplitude_kernel(nv, count_ref, sum_ref, gaps_ref, above_ref, below_ref, swap_ref, out_ref):
    r, parity, g = place()
    owners, _, size, cols = out_ref.shape
    part = size // 2
    slot = (g * size) // nv
    vir = gaps_ref[8:8 + size, :]
    own_gap = gaps_ref[0:1, :]
    own_rows = gaps_ref[2:3, :] - vir
    own_count = count_ref[r]
    lane = lax.broadcasted_iota(jnp.int32, (size, cols), 1)

    def put(j, pair, gap_rows, gap_cols, row_count, col_count):
        keep = (lane < col_count * nv) & (slot < row_count)
        amp = jnp.where(keep, pair / (gap_rows + gap_cols), 0.0).astype(BF)
        for owner in range(out_ref.shape[0]):
            out_ref[owner, j] = amp

    def head(ref, row):
        block = ref[2 * size:, :].astype(F32)
        return block[3 * row:3 * row + 1] + block[3 * row + 1:3 * row + 2] + block[3 * row + 2:3 * row + 3]

    put(0, sum_ref[0:size, :], own_rows, own_gap, own_count, own_count)
    even_count, odd_count = count_ref[r - parity], count_ref[r - parity + 1]
    odd_gap = jnp.where(parity == 0, gaps_ref[1:2, :], own_gap)
    mine = sum_ref[3 * size:, :]
    theirs = swap_ref[size:, :].astype(F32)
    for upper_half in range(2):
        k = (g * part) // nv + upper_half * (cols // nv // 2)
        pair = jnp.where(parity == upper_half, mine, theirs)
        gap_rows = gaps_ref[4 + upper_half:5 + upper_half, :] - gaps_ref[8 + size:, :]
        keep = (lane[:part] < odd_count * nv) & (k < even_count)
        amp = jnp.where(keep, pair / (gap_rows + odd_gap), 0.0).astype(BF)
        for owner in range(owners):
            out_ref[owner, 1, upper_half * part:(upper_half + 1) * part] = amp

    put(
        2, sum_ref[size:2 * size, :] + above_ref[0:size, :].astype(F32), head(above_ref, 2) - vir, own_gap,
        at(count_ref, r + 2), own_count,
    )
    put(
        3, sum_ref[2 * size:3 * size, :] + below_ref[0:size, :].astype(F32), own_rows, head(below_ref, 0),
        own_count, at(count_ref, r - 2),
    )
    other = swap_ref[0:size, :].astype(F32)

    @pl.when(parity == 0)
    def _():
        put(
            4, other + below_ref[size:2 * size, :].astype(F32), own_rows, head(below_ref, 1),
            own_count, at(count_ref, r - 1),
        )

    @pl.when(parity == 1)
    def _():
        put(
            4, other + above_ref[size:2 * size, :].astype(F32), head(above_ref, 3) - vir, own_gap,
            at(count_ref, r + 1), own_count,
        )


def gamma_kernel(
    aux_ref, amps_ref, o_ref, p_ref, n0_ref, n1_ref, m0_ref, m1_ref, x_ref, out_ref, result, weights, sems
):
    rows, cols = o_ref.shape
    half = rows // 2
    _, parity, g = place()

    def put(j, matrix):
        weights[j * cols:(j + 1) * cols, :] = matrix

    def whole(j):
        return amps_ref[:, j].reshape(cols, cols)

    part = amps_ref.shape[2] // 2
    both = jnp.concatenate(
        [amps_ref[:, 1, k * part:(k + 1) * part].reshape(cols // 2, cols) for k in range(2)], axis=0
    )
    put(0, whole(0))
    put(2, whole(2))
    put(3, whole(3).T)

    @pl.when(parity == 0)
    def _():
        put(1, both.T)
        put(4, whole(4).T)

    @pl.when(parity == 1)
    def _():
        put(1, both)
        put(4, whole(4))

    tile = rows // sems.shape[0]
    copies = []
    for j in range(sems.shape[0]):
        start = j * tile
        n_ref, m_ref, low = (n0_ref, m0_ref, start) if start < half else (n1_ref, m1_ref, start - half)
        here, there = pl.ds(start, tile), pl.ds(low, tile)
        blocks = jnp.concatenate(
            [o_ref[here, :], p_ref[here, :], n_ref[there, :], m_ref[there, :], x_ref[here, :]], axis=1
        )
        result[here, :] = keep_rows(mm(blocks, weights[...]), start, aux_ref[g]).astype(result.dtype)
        copy = pltpu.make_async_copy(result.at[here, :], out_ref.at[here, :], sems.at[j])
        copy.start()
        copies.append(copy)
    for copy in copies:
        copy.wait()


def cost(flops, size):
    return pl.CostEstimate(flops=flops, bytes_accessed=size, transcendentals=0)


def memory(mebibytes):
    return pltpu.CompilerParams(vmem_limit_bytes=mebibytes << 20)


def per_device(three_index, occ_energy, vir_energy, aux_count, occ_count):
    rows, cols = three_index.shape
    half = rows // 2
    nv = vir_energy.shape[0]
    slabs = lax.axis_size("blk")
    owners = lax.axis_size("grp")
    piece = cols // owners
    part = piece // 2

    def shift(value, steps):
        return lax.ppermute(value, "blk", [(i, (i + steps) % slabs) for i in range(slabs)])

    def swap(value):
        return lax.ppermute(value, "blk", [(i, i ^ 1) for i in range(slabs)])

    def shape(*dims, dtype=BF):
        return jax.ShapeDtypeStruct(dims, dtype)

    own = three_index
    lower, upper = own[:half], own[half:]
    n0 = shift(lower, -2)
    m1 = shift(upper, 2)
    partner = swap(own)
    partner_energy = swap(occ_energy)

    o0t, o1t, pt, near, gaps, head = pl.pallas_call(
        prep_kernel,
        in_specs=[SM, SM, SM, VM, VM, VM, VM],
        out_specs=[VM] * 6,
        out_shape=[
            shape(cols, half), shape(cols, half), shape(cols, half), shape(owners, piece + part, cols),
            shape(8 + piece + part, cols, dtype=F32), shape(16, cols),
        ],
        cost_estimate=cost(4 * rows * cols * cols, 8 * rows * cols),
        compiler_params=memory(16),
        name="prep",
    )(
        aux_count, occ_energy, partner_energy, vir_energy[None, :],
        jnp.broadcast_to(vir_energy[:, None], (nv, cols)), own, partner,
    )
    upper, lower, near = lax.optimization_barrier((upper, lower, near))
    n1 = shift(upper, -2)
    m0 = shift(lower, 2)
    parts = shape(owners, 4 * piece + part, cols)
    partial_sums = pl.pallas_call(
        far_kernel,
        in_specs=[VM] * 6,
        out_specs=VM,
        out_shape=parts,
        cost_estimate=cost(3 * rows * cols * cols, 5 * rows * cols),
        compiler_params=memory(12),
        name="far",
    )(n0, m1, o0t, o1t, pt, near)
    pieces = lax.all_to_all(partial_sums, "grp", 0, 0)
    message = shape(2 * piece + 16, cols)
    sums, up, down, extra = pl.pallas_call(
        pack_kernel,
        in_specs=[VM, VM],
        out_specs=[VM] * 4,
        out_shape=[shape(3 * piece + part, cols, dtype=F32), message, message, shape(piece + part, cols)],
        cost_estimate=cost(cols * cols, 4 * cols * cols),
        compiler_params=memory(6),
        name="pack",
    )(pieces, head)
    below = shift(up, 2)
    above = shift(down, -2)
    extra = swap(extra)
    amps = pl.pallas_call(
        lambda *refs: amplitude_kernel(nv, *refs),
        in_specs=[SM] + [VM] * 5,
        out_specs=VM,
        out_shape=shape(owners, 5, piece, cols),
        cost_estimate=cost(cols * cols, 8 * cols * cols),
        compiler_params=memory(6),
        name="amplitude",
    )(occ_count, sums, gaps, above, below, extra)
    amps = lax.all_to_all(amps, "grp", 0, 0)
    fifth = swap(jnp.where(
        lax.axis_index("blk") % 2 == 0, jnp.concatenate([n0, n1], axis=0), jnp.concatenate([m0, m1], axis=0)
    ))

    tiles = 8
    return pl.pallas_call(
        gamma_kernel,
        in_specs=[SM] + [VM] * 8,
        out_specs=ANY,
        out_shape=jax.ShapeDtypeStruct((rows, cols), three_index.dtype),
        scratch_shapes=[
            pltpu.VMEM((rows, cols), three_index.dtype), pltpu.VMEM((5 * cols, cols), BF),
            pltpu.SemaphoreType.DMA((tiles,)),
        ],
        cost_estimate=cost(10 * rows * cols * cols, 14 * rows * cols),
        compiler_params=memory(20),
        name="gamma",
    )(aux_count, amps, own, partner, n0, n1, m0, m1, fifth)


def solution(mesh):
    in_specs = (P("grp", "blk"), P("blk"), P(), P(), P())
    out_specs = P("grp", "blk")
    return jax.shard_map(
        per_device, mesh=mesh, in_specs=in_specs, out_specs=out_specs, check_vma=False
    )
```

```python
import jax
import jax.numpy as jnp
from jax import lax
from jax.experimental import pallas as pl
from jax.experimental.pallas import tpu as pltpu
from jax.sharding import PartitionSpec as P


BF = jnp.bfloat16
F32 = jnp.float32
VM = pl.BlockSpec(memory_space=pltpu.VMEM)
SM = pl.BlockSpec(memory_space=pltpu.SMEM)
ANY = pl.BlockSpec(memory_space=pl.ANY)


def mm(a, b):
    return jnp.dot(a, b, preferred_element_type=F32)


def keep_rows(block, start, count):
    row = lax.broadcasted_iota(jnp.int32, block.shape, 0) + start
    return jnp.where(row < count, block, jnp.zeros((), block.dtype))


def place():
    r = lax.axis_index("blk")
    return r, lax.rem(r, 2), lax.axis_index("grp")


def at(count_ref, index):
    slabs = count_ref.shape[0]
    return count_ref[lax.rem(index + slabs, slabs)]


def three_terms(value):
    hi = value.astype(BF)
    rest = value - hi.astype(F32)
    mid = rest.astype(BF)
    low = (rest - mid.astype(F32)).astype(BF)
    return [hi.astype(F32), mid.astype(F32), low.astype(F32)]


def prep_kernel(
    aux_ref, energy_ref, other_ref, vir_ref, vir_rows_ref, own_ref, p_ref,
    o0t_ref, o1t_ref, pt_ref, near_ref, gaps_ref, head_ref,
):
    _, parity, g = place()
    rows, cols = own_ref.shape
    half = rows // 2
    owners = near_ref.shape[0]
    piece = cols // owners
    part = piece // 2
    nv = vir_ref.shape[1]
    count = aux_ref[g]
    o0t_ref[...] = keep_rows(own_ref[:half, :], 0, count).T
    o1t_ref[...] = keep_rows(own_ref[half:, :], half, count).T

    @pl.when(parity == 0)
    def _():
        pt_ref[...] = keep_rows(p_ref[:half, :], 0, count).T

    @pl.when(parity == 1)
    def _():
        pt_ref[...] = keep_rows(p_ref[half:, :], half, count).T

    def put(rows_of, pair):
        near_ref[:, rows_of] = pair.reshape(owners, pair.shape[0] // owners, cols).astype(BF)

    put(slice(0, piece), mm(o0t_ref[...], own_ref[:half, :]) + mm(o1t_ref[...], own_ref[half:, :]))
    middle = cols // 2

    @pl.when(parity == 0)
    def _():
        put(
            slice(piece, piece + part),
            mm(o0t_ref[:middle, :], p_ref[:half, :]) + mm(o1t_ref[:middle, :], p_ref[half:, :]),
        )

    @pl.when(parity == 1)
    def _():
        low = keep_rows(p_ref[:half, middle:], 0, count).T
        put(
            slice(piece, piece + part),
            mm(low, own_ref[:half, :]) + mm(pt_ref[middle:, :], own_ref[half:, :]),
        )

    slots = cols // nv
    slot = (g * piece) // nv
    lane = lax.broadcasted_iota(jnp.int32, (1, cols), 1)
    vir = jnp.concatenate([vir_ref[...]] * slots, axis=1)
    rows_out = []
    for ref in (energy_ref, other_ref):
        level = jnp.zeros((1, cols), F32)
        for k in range(slots):
            level = jnp.where(lane // nv == k, ref[k], level)
        rows_out.append(level - vir)
    for ref in (energy_ref, other_ref):
        rows_out.append(jnp.broadcast_to(ref[slot], (1, cols)))
    terms = []
    for row in rows_out:
        terms += three_terms(row)
    zero = jnp.zeros((4, cols), F32)
    head_ref[...] = jnp.concatenate(terms + [zero], axis=0).astype(BF)
    for upper_half in range(2):
        k = (g * part) // nv + upper_half * (slots // 2)
        level = jnp.where(parity == 0, energy_ref[k], other_ref[k])
        rows_out.append(jnp.broadcast_to(level, (1, cols)))
    gaps_ref[0:8, :] = jnp.concatenate(rows_out + [zero[:2]], axis=0)
    start = pl.multiple_of(lax.rem(g * piece, nv), piece)
    gaps_ref[8:8 + piece, :] = vir_rows_ref[pl.ds(start, piece), :]
    start = pl.multiple_of(lax.rem(g * part, nv), part)
    gaps_ref[8 + piece:, :] = vir_rows_ref[pl.ds(start, part), :]


def far_kernel(n_ref, m_ref, o0t_ref, o1t_ref, pt_ref, near_ref, out_ref):
    _, parity, _ = place()
    owners, _, cols = out_ref.shape
    piece = cols // owners
    near = near_ref.shape[1]

    def put(j, pair):
        out_ref[:, near + j * piece:near + (j + 1) * piece] = pair.reshape(owners, piece, cols).astype(BF)

    out_ref[:, 0:near] = near_ref[...]
    put(0, mm(o0t_ref[...], n_ref[...]).T)
    put(1, mm(o1t_ref[...], m_ref[...]))

    @pl.when(parity == 0)
    def _():
        put(2, mm(pt_ref[...], n_ref[...]).T)

    @pl.when(parity == 1)
    def _():
        put(2, mm(pt_ref[...], m_ref[...]))


def pack_kernel(parts_ref, head_ref, sum_ref, up_ref, down_ref, swap_ref):
    total = jnp.sum(parts_ref[...].astype(F32), axis=0)
    size = parts_ref.shape[2] // parts_ref.shape[0]
    part = size // 2
    near = size + part
    sum_ref[0:size, :] = total[0:size]
    sum_ref[size:3 * size, :] = total[near:near + 2 * size]
    sum_ref[3 * size:, :] = total[size:near]
    extra = total[near + 2 * size:].astype(BF)
    swap_ref[0:size, :] = extra
    swap_ref[size:, :] = total[size:near].astype(BF)
    for j, ref in ((0, up_ref), (1, down_ref)):
        ref[0:size, :] = total[near + j * size:near + (j + 1) * size].astype(BF)
        ref[size:2 * size, :] = extra
        ref[2 * size:, :] = head_ref[...]


def amplitude_kernel(nv, count_ref, sum_ref, gaps_ref, above_ref, below_ref, swap_ref, out_ref):
    r, parity, g = place()
    owners, _, size, cols = out_ref.shape
    part = size // 2
    slot = (g * size) // nv
    vir = gaps_ref[8:8 + size, :]
    own_gap = gaps_ref[0:1, :]
    own_rows = gaps_ref[2:3, :] - vir
    own_count = count_ref[r]
    lane = lax.broadcasted_iota(jnp.int32, (size, cols), 1)

    def put(j, pair, gap_rows, gap_cols, row_count, col_count):
        keep = (lane < col_count * nv) & (slot < row_count)
        amp = jnp.where(keep, pair / (gap_rows + gap_cols), 0.0).astype(BF)
        for owner in range(out_ref.shape[0]):
            out_ref[owner, j] = amp

    def head(ref, row):
        block = ref[2 * size:, :].astype(F32)
        return block[3 * row:3 * row + 1] + block[3 * row + 1:3 * row + 2] + block[3 * row + 2:3 * row + 3]

    put(0, sum_ref[0:size, :], own_rows, own_gap, own_count, own_count)
    even_count, odd_count = count_ref[r - parity], count_ref[r - parity + 1]
    odd_gap = jnp.where(parity == 0, gaps_ref[1:2, :], own_gap)
    mine = sum_ref[3 * size:, :]
    theirs = swap_ref[size:, :].astype(F32)
    for upper_half in range(2):
        k = (g * part) // nv + upper_half * (cols // nv // 2)
        pair = jnp.where(parity == upper_half, mine, theirs)
        gap_rows = gaps_ref[4 + upper_half:5 + upper_half, :] - gaps_ref[8 + size:, :]
        keep = (lane[:part] < odd_count * nv) & (k < even_count)
        amp = jnp.where(keep, pair / (gap_rows + odd_gap), 0.0).astype(BF)
        for owner in range(owners):
            out_ref[owner, 1, upper_half * part:(upper_half + 1) * part] = amp

    put(
        2, sum_ref[size:2 * size, :] + above_ref[0:size, :].astype(F32), head(above_ref, 2) - vir, own_gap,
        at(count_ref, r + 2), own_count,
    )
    put(
        3, sum_ref[2 * size:3 * size, :] + below_ref[0:size, :].astype(F32), own_rows, head(below_ref, 0),
        own_count, at(count_ref, r - 2),
    )
    other = swap_ref[0:size, :].astype(F32)

    @pl.when(parity == 0)
    def _():
        put(
            4, other + below_ref[size:2 * size, :].astype(F32), own_rows, head(below_ref, 1),
            own_count, at(count_ref, r - 1),
        )

    @pl.when(parity == 1)
    def _():
        put(
            4, other + above_ref[size:2 * size, :].astype(F32), head(above_ref, 3) - vir, own_gap,
            at(count_ref, r + 1), own_count,
        )


def gamma_kernel(
    aux_ref, amps_ref, o_ref, p_ref, n0_ref, n1_ref, m0_ref, m1_ref, x_ref, out_ref,
    n_buf, m_buf, x_buf, result, weights, sems,
):
    rows, cols = o_ref.shape
    half = rows // 2
    tiles = sems.shape[1]
    tile = rows // tiles
    fetches = []
    for j in range(tiles):
        start = j * tile
        here, low = pl.ds(start, tile), pl.ds(start % half, tile)
        wanted = [(x_ref.at[here, :], x_buf.at[here, :])]
        wanted.append((m0_ref.at[low, :], m_buf.at[low, :]) if start < half else (n1_ref.at[low, :], n_buf.at[low, :]))
        fetches.append([pltpu.make_async_copy(src, dst, sems.at[k, j]) for k, (src, dst) in enumerate(wanted)])
        for copy in fetches[j]:
            copy.start()
    _, parity, g = place()

    def put(j, matrix):
        weights[j * cols:(j + 1) * cols, :] = matrix

    def whole(j):
        return amps_ref[:, j].reshape(cols, cols)

    part = amps_ref.shape[2] // 2
    both = jnp.concatenate(
        [amps_ref[:, 1, k * part:(k + 1) * part].reshape(cols // 2, cols) for k in range(2)], axis=0
    )
    put(0, whole(0))
    put(2, whole(2))
    put(3, whole(3).T)

    @pl.when(parity == 0)
    def _():
        put(1, both.T)
        put(4, whole(4).T)

    @pl.when(parity == 1)
    def _():
        put(1, both)
        put(4, whole(4))

    copies = []
    for j in range(tiles):
        start = j * tile
        n_ref, m_ref = (n0_ref, m_buf) if start < half else (n_buf, m1_ref)
        here, low = pl.ds(start, tile), pl.ds(start % half, tile)
        for copy in fetches[j]:
            copy.wait()
        blocks = jnp.concatenate(
            [o_ref[here, :], p_ref[here, :], n_ref[low, :], m_ref[low, :], x_buf[here, :]], axis=1
        )
        result[here, :] = keep_rows(mm(blocks, weights[...]), start, aux_ref[g]).astype(result.dtype)
        copy = pltpu.make_async_copy(result.at[here, :], out_ref.at[here, :], sems.at[2, j])
        copy.start()
        copies.append(copy)
    for copy in copies:
        copy.wait()


def cost(flops, size):
    return pl.CostEstimate(flops=flops, bytes_accessed=size, transcendentals=0)


def memory(mebibytes):
    return pltpu.CompilerParams(vmem_limit_bytes=mebibytes << 20)


def per_device(three_index, occ_energy, vir_energy, aux_count, occ_count):
    rows, cols = three_index.shape
    half = rows // 2
    nv = vir_energy.shape[0]
    slabs = lax.axis_size("blk")
    owners = lax.axis_size("grp")
    piece = cols // owners
    part = piece // 2

    def shift(value, steps):
        return lax.ppermute(value, "blk", [(i, (i + steps) % slabs) for i in range(slabs)])

    def swap(value):
        return lax.ppermute(value, "blk", [(i, i ^ 1) for i in range(slabs)])

    def shape(*dims, dtype=BF):
        return jax.ShapeDtypeStruct(dims, dtype)

    own = three_index
    lower, upper = own[:half], own[half:]
    n0 = shift(lower, -2)
    m1 = shift(upper, 2)
    partner = swap(own)
    partner_energy = swap(occ_energy)

    o0t, o1t, pt, near, gaps, head = pl.pallas_call(
        prep_kernel,
        in_specs=[SM, SM, SM, VM, VM, VM, VM],
        out_specs=[VM] * 6,
        out_shape=[
            shape(cols, half), shape(cols, half), shape(cols, half), shape(owners, piece + part, cols),
            shape(8 + piece + part, cols, dtype=F32), shape(16, cols),
        ],
        cost_estimate=cost(4 * rows * cols * cols, 8 * rows * cols),
        compiler_params=memory(16),
        name="prep",
    )(
        aux_count, occ_energy, partner_energy, vir_energy[None, :],
        jnp.broadcast_to(vir_energy[:, None], (nv, cols)), own, partner,
    )
    upper, lower, near = lax.optimization_barrier((upper, lower, near))
    n1 = shift(upper, -2)
    m0 = shift(lower, 2)
    parts = shape(owners, 4 * piece + part, cols)
    partial_sums = pl.pallas_call(
        far_kernel,
        in_specs=[VM] * 6,
        out_specs=VM,
        out_shape=parts,
        cost_estimate=cost(3 * rows * cols * cols, 5 * rows * cols),
        compiler_params=memory(12),
        name="far",
    )(n0, m1, o0t, o1t, pt, near)
    pieces = lax.all_to_all(partial_sums, "grp", 0, 0)
    message = shape(2 * piece + 16, cols)
    sums, up, down, extra = pl.pallas_call(
        pack_kernel,
        in_specs=[VM, VM],
        out_specs=[VM] * 4,
        out_shape=[shape(3 * piece + part, cols, dtype=F32), message, message, shape(piece + part, cols)],
        cost_estimate=cost(cols * cols, 4 * cols * cols),
        compiler_params=memory(6),
        name="pack",
    )(pieces, head)
    below = shift(up, 2)
    above = shift(down, -2)
    extra = swap(extra)
    amps = pl.pallas_call(
        lambda *refs: amplitude_kernel(nv, *refs),
        in_specs=[SM] + [VM] * 5,
        out_specs=VM,
        out_shape=shape(owners, 5, piece, cols),
        cost_estimate=cost(cols * cols, 8 * cols * cols),
        compiler_params=memory(6),
        name="amplitude",
    )(occ_count, sums, gaps, above, below, extra)
    amps = lax.all_to_all(amps, "grp", 0, 0)
    fifth = swap(jnp.where(
        lax.axis_index("blk") % 2 == 0, jnp.concatenate([n0, n1], axis=0), jnp.concatenate([m0, m1], axis=0)
    ))

    tiles = 8
    return pl.pallas_call(
        gamma_kernel,
        in_specs=[SM, VM, VM, VM, VM, ANY, ANY, VM, ANY],
        out_specs=ANY,
        out_shape=jax.ShapeDtypeStruct((rows, cols), three_index.dtype),
        scratch_shapes=[
            pltpu.VMEM((half, cols), BF), pltpu.VMEM((half, cols), BF), pltpu.VMEM((rows, cols), BF),
            pltpu.VMEM((rows, cols), three_index.dtype), pltpu.VMEM((5 * cols, cols), BF),
            pltpu.SemaphoreType.DMA((3, tiles)),
        ],
        cost_estimate=cost(10 * rows * cols * cols, 14 * rows * cols),
        compiler_params=memory(20),
        name="gamma",
    )(aux_count, amps, own, partner, n0, n1, m0, m1, fifth)


def solution(mesh):
    in_specs = (P("grp", "blk"), P("blk"), P(), P(), P())
    out_specs = P("grp", "blk")
    return jax.shard_map(
        per_device, mesh=mesh, in_specs=in_specs, out_specs=out_specs, check_vma=False
    )
```

```python
import jax
import jax.numpy as jnp
from jax import lax
from jax.experimental import pallas as pl
from jax.experimental.pallas import tpu as pltpu
from jax.sharding import PartitionSpec as P


BF = jnp.bfloat16
F32 = jnp.float32
VM = pl.BlockSpec(memory_space=pltpu.VMEM)
SM = pl.BlockSpec(memory_space=pltpu.SMEM)
ANY = pl.BlockSpec(memory_space=pl.ANY)


def mm(a, b):
    return jnp.dot(a, b, preferred_element_type=F32)


def keep_rows(block, start, count):
    row = lax.broadcasted_iota(jnp.int32, block.shape, 0) + start
    return jnp.where(row < count, block, jnp.zeros((), block.dtype))


def place():
    r = lax.axis_index("blk")
    return r, lax.rem(r, 2), lax.axis_index("grp")


def at(count_ref, index):
    slabs = count_ref.shape[0]
    return count_ref[lax.rem(index + slabs, slabs)]


def three_terms(value):
    hi = value.astype(BF)
    rest = value - hi.astype(F32)
    mid = rest.astype(BF)
    low = (rest - mid.astype(F32)).astype(BF)
    return [hi.astype(F32), mid.astype(F32), low.astype(F32)]


def prep_kernel(
    aux_ref, energy_ref, other_ref, vir_ref, vir_rows_ref, own_ref, p_ref,
    ot_ref, pt_ref, near_ref, gaps_ref, head_ref,
):
    _, parity, g = place()
    cols = own_ref.shape[1]
    middle = cols // 2
    owners = near_ref.shape[0]
    piece = cols // owners
    part = piece // 2
    nv = vir_ref.shape[1]
    count = aux_ref[g]
    ot_ref[...] = keep_rows(own_ref[...], 0, count).T
    pt_ref[...] = keep_rows(p_ref[...], 0, count).T

    def put(rows_of, pair):
        near_ref[:, rows_of] = pair.reshape(owners, pair.shape[0] // owners, cols).astype(BF)

    put(slice(0, piece), mm(ot_ref[...], own_ref[...]))

    @pl.when(parity == 0)
    def _():
        put(slice(piece, piece + part), mm(ot_ref[:middle, :], p_ref[...]))

    @pl.when(parity == 1)
    def _():
        put(slice(piece, piece + part), mm(pt_ref[middle:, :], own_ref[...]))

    slots = cols // nv
    slot = (g * piece) // nv
    k = (g * part) // nv
    vir = jnp.concatenate([vir_ref[...]] * slots, axis=1)

    def spread(value):
        return jnp.broadcast_to(value, (1, cols))

    own_gap = levels(energy_ref, nv, cols) - vir
    other_gap = levels(other_ref, nv, cols) - vir
    own_level = spread(energy_ref[slot])
    own_parts = [energy_ref[k], energy_ref[k + slots // 2]]
    other_parts = [other_ref[k], other_ref[k + slots // 2]]
    even_parts = [jnp.where(parity == 0, a, b) for a, b in zip(own_parts, other_parts)]
    terms = []
    for row in [own_gap, other_gap, own_level] + [spread(value) for value in other_parts]:
        terms += three_terms(row)
    head_ref[...] = jnp.concatenate(terms + [jnp.zeros((1, cols), F32)], axis=0).astype(BF)
    gaps_ref[0:8, :] = jnp.concatenate(
        [own_gap, other_gap, own_level, vir] + [spread(value) for value in even_parts + own_parts], axis=0
    )
    start = pl.multiple_of(lax.rem(g * piece, nv), piece)
    gaps_ref[8:8 + piece, :] = vir_rows_ref[pl.ds(start, piece), :]
    start = pl.multiple_of(lax.rem(g * part, nv), part)
    gaps_ref[8 + piece:, :] = vir_rows_ref[pl.ds(start, part), :]


def levels(energy_ref, nv, cols):
    lane = lax.broadcasted_iota(jnp.int32, (1, cols), 1)
    level = jnp.zeros((1, cols), F32)
    for k in range(cols // nv):
        level = jnp.where(lane // nv == k, energy_ref[k], level)
    return level


def far_kernel(f_ref, ot_ref, pt_ref, near_ref, out_ref):
    _, parity, _ = place()
    owners, _, cols = out_ref.shape
    middle = cols // 2
    near = near_ref.shape[1]
    piece = cols // owners
    out_ref[:, 0:near] = near_ref[...]
    out_ref[:, near:near + piece] = mm(ot_ref[...], f_ref[...]).reshape(owners, piece, cols).astype(BF)

    def put(pair):
        out_ref[:, near + piece:] = pair.reshape(owners, piece // 2, cols).astype(BF)

    @pl.when(parity == 0)
    def _():
        put(mm(pt_ref[:middle, :], f_ref[...]))

    @pl.when(parity == 1)
    def _():
        put(mm(pt_ref[...], f_ref[:, middle:]).T)


def pack_kernel(parts_ref, head_ref, sum_ref, message_ref, swap_ref):
    total = jnp.sum(parts_ref[...].astype(F32), axis=0)
    size = parts_ref.shape[2] // parts_ref.shape[0]
    part = size // 2
    near = size + part
    across = total[near + size:].astype(BF)
    sum_ref[...] = total[:near + size]
    message_ref[0:size, :] = total[near:near + size].astype(BF)
    message_ref[size:near, :] = across
    message_ref[near:, :] = head_ref[...]
    swap_ref[0:part, :] = across
    swap_ref[part:, :] = total[size:near].astype(BF)


def amplitude_kernel(nv, count_ref, energy_ref, sum_ref, gaps_ref, message_ref, swap_ref, out_ref):
    r, parity, g = place()
    owners, _, size, cols = out_ref.shape
    part = size // 2
    near = size + part
    slot = (g * size) // nv
    sign = 1 - 2 * parity
    vir = gaps_ref[8:8 + size, :]
    vir_part = gaps_ref[8 + size:, :]
    own_gap = gaps_ref[0:1, :]
    own_rows = gaps_ref[2:3, :] - vir
    own_count, p_count = count_ref[r], count_ref[r + sign]
    f_count, s_count, x_count = at(count_ref, r + 2 * sign), at(count_ref, r - 2 * sign), at(count_ref, r - sign)
    lane = lax.broadcasted_iota(jnp.int32, (size, cols), 1)

    def head(row):
        block = message_ref[near:, :].astype(F32)
        return block[3 * row:3 * row + 1] + block[3 * row + 1:3 * row + 2] + block[3 * row + 2:3 * row + 3]

    def put(j, rows, pair, gap_rows, gap_cols, row_live, col_count):
        keep = (lane[:pair.shape[0]] < col_count * nv) & row_live
        amp = jnp.where(keep, pair / (gap_rows + gap_cols), 0.0).astype(BF)
        for owner in range(owners):
            out_ref[owner, j, rows] = amp

    every = slice(0, size)
    put(0, every, sum_ref[0:size, :], own_rows, own_gap, slot < own_count, own_count)
    f_gap = levels(energy_ref, nv, cols) - gaps_ref[3:4, :]
    put(2, every, sum_ref[near:, :], own_rows, f_gap, slot < own_count, f_count)
    put(3, every, message_ref[0:size, :].astype(F32), head(2) - vir, own_gap, slot < s_count, own_count)

    even = parity == 0
    even_count, odd_count = jnp.where(even, own_count, p_count), jnp.where(even, p_count, own_count)
    odd_gap = jnp.where(even, gaps_ref[1:2, :], own_gap)
    row_count, col_count = jnp.where(even, x_count, own_count), jnp.where(even, own_count, x_count)
    col_gap = jnp.where(even, own_gap, head(1))
    for h in range(2):
        k = (g * part) // nv + h * (cols // nv // 2)
        rows = slice(h * part, (h + 1) * part)
        pair = jnp.where(parity == h, sum_ref[size:near, :], swap_ref[part:, :].astype(F32))
        put(1, rows, pair, gaps_ref[4 + h:5 + h, :] - vir_part, odd_gap, k < even_count, odd_count)
        pair = jnp.where(parity == h, message_ref[size:near, :].astype(F32), swap_ref[0:part, :].astype(F32))
        level = jnp.where(even, head(3 + h), gaps_ref[6 + h:7 + h, :])
        put(4, rows, pair, level - vir_part, col_gap, k < row_count, col_count)


def gamma_kernel(aux_ref, amps_ref, o_ref, p_ref, f_ref, s_ref, x_ref, out_ref, result, weights, sems):
    rows, cols = o_ref.shape
    _, parity, g = place()

    def put(j, matrix):
        weights[j * cols:(j + 1) * cols, :] = matrix

    def whole(j):
        return amps_ref[:, j].reshape(cols, cols)

    def halves(j):
        part = amps_ref.shape[2] // 2
        return jnp.concatenate(
            [amps_ref[:, j, h * part:(h + 1) * part].reshape(cols // 2, cols) for h in range(2)], axis=0
        )

    put(0, whole(0))
    put(2, whole(2).T)
    put(3, whole(3))

    @pl.when(parity == 0)
    def _():
        put(1, halves(1).T)
        put(4, halves(4))

    @pl.when(parity == 1)
    def _():
        put(1, halves(1))
        put(4, halves(4).T)

    tile = rows // sems.shape[0]
    copies = []
    for j in range(sems.shape[0]):
        here = pl.ds(j * tile, tile)
        blocks = jnp.concatenate([ref[here, :] for ref in (o_ref, p_ref, f_ref, s_ref, x_ref)], axis=1)
        result[here, :] = keep_rows(mm(blocks, weights[...]), j * tile, aux_ref[g]).astype(result.dtype)
        copy = pltpu.make_async_copy(result.at[here, :], out_ref.at[here, :], sems.at[j])
        copy.start()
        copies.append(copy)
    for copy in copies:
        copy.wait()


def cost(flops, size):
    return pl.CostEstimate(flops=flops, bytes_accessed=size, transcendentals=0)


def memory(mebibytes):
    return pltpu.CompilerParams(vmem_limit_bytes=mebibytes << 20)


def per_device(three_index, occ_energy, vir_energy, aux_count, occ_count):
    rows, cols = three_index.shape
    nv = vir_energy.shape[0]
    slabs = lax.axis_size("blk")
    owners = lax.axis_size("grp")
    piece = cols // owners
    part = piece // 2

    def across(value, steps):
        pairs = [(i, (i + (steps if i % 2 == 0 else -steps)) % slabs) for i in range(slabs)]
        return lax.ppermute(value, "blk", pairs)

    def swap(value):
        return lax.ppermute(value, "blk", [(i, i ^ 1) for i in range(slabs)])

    def shape(*dims, dtype=BF):
        return jax.ShapeDtypeStruct(dims, dtype)

    own = three_index
    f_block = across(own, -2)
    partner = swap(own)
    partner_energy = swap(occ_energy)
    f_energy = across(occ_energy, -2)

    ot, pt, near, gaps, head = pl.pallas_call(
        prep_kernel,
        in_specs=[SM, SM, SM, VM, VM, VM, VM],
        out_specs=[VM] * 5,
        out_shape=[
            shape(cols, rows), shape(cols, rows), shape(owners, piece + part, cols),
            shape(8 + piece + part, cols, dtype=F32), shape(16, cols),
        ],
        cost_estimate=cost(3 * rows * cols * cols, 8 * rows * cols),
        compiler_params=memory(20),
        name="prep",
    )(
        aux_count, occ_energy, partner_energy, vir_energy[None, :],
        jnp.broadcast_to(vir_energy[:, None], (nv, cols)), own, partner,
    )
    own_later, near, f_energy = lax.optimization_barrier((own, near, f_energy))
    s_block = across(own_later, 2)
    parts = shape(owners, 3 * piece, cols)
    partial_sums = pl.pallas_call(
        far_kernel,
        in_specs=[VM] * 4,
        out_specs=VM,
        out_shape=parts,
        cost_estimate=cost(3 * rows * cols * cols, 5 * rows * cols),
        compiler_params=memory(12),
        name="far",
    )(f_block, ot, pt, near)
    pieces = lax.all_to_all(partial_sums, "grp", 0, 0)
    sums, message, extra = pl.pallas_call(
        pack_kernel,
        in_specs=[VM, VM],
        out_specs=[VM] * 3,
        out_shape=[
            shape(2 * piece + part, cols, dtype=F32), shape(piece + part + 16, cols), shape(piece, cols),
        ],
        cost_estimate=cost(cols * cols, 4 * cols * cols),
        compiler_params=memory(6),
        name="pack",
    )(pieces, head)
    fifth = swap(f_block)
    message, s_block, fifth = lax.optimization_barrier((message, s_block, fifth))
    message = across(message, 2)
    extra = swap(extra)
    amps = pl.pallas_call(
        lambda *refs: amplitude_kernel(nv, *refs),
        in_specs=[SM, SM] + [VM] * 4,
        out_specs=VM,
        out_shape=shape(owners, 5, piece, cols),
        cost_estimate=cost(cols * cols, 8 * cols * cols),
        compiler_params=memory(6),
        name="amplitude",
    )(occ_count, f_energy, sums, gaps, message, extra)
    amps = lax.all_to_all(amps, "grp", 0, 0)

    tiles = 8
    return pl.pallas_call(
        gamma_kernel,
        in_specs=[SM] + [VM] * 6,
        out_specs=ANY,
        out_shape=jax.ShapeDtypeStruct((rows, cols), three_index.dtype),
        scratch_shapes=[
            pltpu.VMEM((rows, cols), three_index.dtype), pltpu.VMEM((5 * cols, cols), BF),
            pltpu.SemaphoreType.DMA((tiles,)),
        ],
        cost_estimate=cost(10 * rows * cols * cols, 14 * rows * cols),
        compiler_params=memory(20),
        name="gamma",
    )(aux_count, amps, own, partner, f_block, s_block, fifth)


def solution(mesh):
    in_specs = (P("grp", "blk"), P("blk"), P(), P(), P())
    out_specs = P("grp", "blk")
    return jax.shard_map(
        per_device, mesh=mesh, in_specs=in_specs, out_specs=out_specs, check_vma=False
    )
```

```python
import jax
import jax.numpy as jnp
from jax import lax
from jax.experimental import pallas as pl
from jax.experimental.pallas import tpu as pltpu
from jax.sharding import PartitionSpec as P


BF = jnp.bfloat16
F32 = jnp.float32
VM = pl.BlockSpec(memory_space=pltpu.VMEM)
SM = pl.BlockSpec(memory_space=pltpu.SMEM)
ANY = pl.BlockSpec(memory_space=pl.ANY)


def mm(a, b):
    return jnp.dot(a, b, preferred_element_type=F32)


def keep_rows(block, start, count):
    row = lax.broadcasted_iota(jnp.int32, block.shape, 0) + start
    return jnp.where(row < count, block, jnp.zeros((), block.dtype))


def place():
    r = lax.axis_index("blk")
    return r, lax.rem(r, 2), lax.axis_index("grp")


def at(count_ref, index):
    slabs = count_ref.shape[0]
    return count_ref[lax.rem(index + slabs, slabs)]


def three_terms(value):
    hi = value.astype(BF)
    rest = value - hi.astype(F32)
    mid = rest.astype(BF)
    low = (rest - mid.astype(F32)).astype(BF)
    return [hi.astype(F32), mid.astype(F32), low.astype(F32)]


def prep_kernel(
    aux_ref, energy_ref, other_ref, vir_ref, vir_rows_ref, own_ref, p_ref,
    ot_ref, pt_ref, near_ref, gaps_ref, head_ref,
):
    _, parity, g = place()
    cols = own_ref.shape[1]
    middle = cols // 2
    owners = near_ref.shape[0]
    piece = cols // owners
    part = piece // 2
    nv = vir_ref.shape[1]
    count = aux_ref[g]
    ot_ref[...] = keep_rows(own_ref[...], 0, count).T
    pt_ref[...] = keep_rows(p_ref[...], 0, count).T

    def put(rows_of, pair):
        near_ref[:, rows_of] = pair.reshape(owners, pair.shape[0] // owners, cols).astype(BF)

    put(slice(0, piece), mm(ot_ref[...], own_ref[...]))

    @pl.when(parity == 0)
    def _():
        put(slice(piece, piece + part), mm(ot_ref[:middle, :], p_ref[...]))

    @pl.when(parity == 1)
    def _():
        put(slice(piece, piece + part), mm(pt_ref[middle:, :], own_ref[...]))

    slots = cols // nv
    slot = (g * piece) // nv
    k = (g * part) // nv
    vir = jnp.concatenate([vir_ref[...]] * slots, axis=1)

    def spread(value):
        return jnp.broadcast_to(value, (1, cols))

    own_gap = levels(energy_ref, nv, cols) - vir
    other_gap = levels(other_ref, nv, cols) - vir
    own_level = spread(energy_ref[slot])
    own_parts = [energy_ref[k], energy_ref[k + slots // 2]]
    other_parts = [other_ref[k], other_ref[k + slots // 2]]
    even_parts = [jnp.where(parity == 0, a, b) for a, b in zip(own_parts, other_parts)]
    terms = []
    for row in [own_gap, other_gap, own_level] + [spread(value) for value in other_parts]:
        terms += three_terms(row)
    head_ref[...] = jnp.concatenate(terms + [jnp.zeros((1, cols), F32)], axis=0).astype(BF)
    gaps_ref[0:8, :] = jnp.concatenate(
        [own_gap, other_gap, own_level, vir] + [spread(value) for value in even_parts + own_parts], axis=0
    )
    start = pl.multiple_of(lax.rem(g * piece, nv), piece)
    gaps_ref[8:8 + piece, :] = vir_rows_ref[pl.ds(start, piece), :]
    start = pl.multiple_of(lax.rem(g * part, nv), part)
    gaps_ref[8 + piece:, :] = vir_rows_ref[pl.ds(start, part), :]


def levels(energy_ref, nv, cols):
    lane = lax.broadcasted_iota(jnp.int32, (1, cols), 1)
    level = jnp.zeros((1, cols), F32)
    for k in range(cols // nv):
        level = jnp.where(lane // nv == k, energy_ref[k], level)
    return level


def far_kernel(f_ref, ot_ref, pt_ref, near_ref, out_ref):
    _, parity, _ = place()
    owners, _, cols = out_ref.shape
    middle = cols // 2
    near = near_ref.shape[1]
    piece = cols // owners
    out_ref[:, 0:near] = near_ref[...]
    out_ref[:, near:near + piece] = mm(ot_ref[...], f_ref[...]).reshape(owners, piece, cols).astype(BF)

    def put(pair):
        out_ref[:, near + piece:] = pair.reshape(owners, piece // 2, cols).astype(BF)

    @pl.when(parity == 0)
    def _():
        put(mm(pt_ref[:middle, :], f_ref[...]))

    @pl.when(parity == 1)
    def _():
        put(mm(pt_ref[...], f_ref[:, middle:]).T)


def pack_kernel(parts_ref, head_ref, sum_ref, message_ref, swap_ref):
    total = jnp.sum(parts_ref[...].astype(F32), axis=0)
    size = parts_ref.shape[2] // parts_ref.shape[0]
    part = size // 2
    near = size + part
    across = total[near + size:].astype(BF)
    sum_ref[...] = total[:near + size]
    message_ref[0:size, :] = total[near:near + size].astype(BF)
    message_ref[size:near, :] = across
    message_ref[near:, :] = head_ref[...]
    swap_ref[0:part, :] = across
    swap_ref[part:, :] = total[size:near].astype(BF)


def amplitude_kernel(nv, count_ref, energy_ref, sum_ref, gaps_ref, message_ref, swap_ref, out_ref):
    r, parity, g = place()
    owners, _, size, cols = out_ref.shape
    part = size // 2
    near = size + part
    slot = (g * size) // nv
    sign = 1 - 2 * parity
    vir = gaps_ref[8:8 + size, :]
    vir_part = gaps_ref[8 + size:, :]
    own_gap = gaps_ref[0:1, :]
    own_rows = gaps_ref[2:3, :] - vir
    own_count, p_count = count_ref[r], count_ref[r + sign]
    f_count, s_count, x_count = at(count_ref, r + 2 * sign), at(count_ref, r - 2 * sign), at(count_ref, r - sign)
    lane = lax.broadcasted_iota(jnp.int32, (size, cols), 1)

    def head(row):
        block = message_ref[near:, :].astype(F32)
        return block[3 * row:3 * row + 1] + block[3 * row + 1:3 * row + 2] + block[3 * row + 2:3 * row + 3]

    def put(j, rows, pair, gap_rows, gap_cols, row_live, col_count):
        keep = (lane[:pair.shape[0]] < col_count * nv) & row_live
        amp = jnp.where(keep, pair / (gap_rows + gap_cols), 0.0).astype(BF)
        for owner in range(owners):
            out_ref[owner, j, rows] = amp

    every = slice(0, size)
    put(0, every, sum_ref[0:size, :], own_rows, own_gap, slot < own_count, own_count)
    f_gap = levels(energy_ref, nv, cols) - gaps_ref[3:4, :]
    put(2, every, sum_ref[near:, :], own_rows, f_gap, slot < own_count, f_count)
    put(3, every, message_ref[0:size, :].astype(F32), head(2) - vir, own_gap, slot < s_count, own_count)

    even = parity == 0
    even_count, odd_count = jnp.where(even, own_count, p_count), jnp.where(even, p_count, own_count)
    odd_gap = jnp.where(even, gaps_ref[1:2, :], own_gap)
    row_count, col_count = jnp.where(even, x_count, own_count), jnp.where(even, own_count, x_count)
    col_gap = jnp.where(even, own_gap, head(1))
    for h in range(2):
        k = (g * part) // nv + h * (cols // nv // 2)
        rows = slice(h * part, (h + 1) * part)
        pair = jnp.where(parity == h, sum_ref[size:near, :], swap_ref[part:, :].astype(F32))
        put(1, rows, pair, gaps_ref[4 + h:5 + h, :] - vir_part, odd_gap, k < even_count, odd_count)
        pair = jnp.where(parity == h, message_ref[size:near, :].astype(F32), swap_ref[0:part, :].astype(F32))
        level = jnp.where(even, head(3 + h), gaps_ref[6 + h:7 + h, :])
        put(4, rows, pair, level - vir_part, col_gap, k < row_count, col_count)


def gamma_kernel(aux_ref, amps_ref, o_ref, p_ref, f_ref, s_ref, x_ref, out_ref, result, weights, sems):
    rows, cols = o_ref.shape
    _, parity, g = place()

    def put(j, matrix):
        weights[j * cols:(j + 1) * cols, :] = matrix

    def whole(j):
        return amps_ref[:, j].reshape(cols, cols)

    def halves(j):
        part = amps_ref.shape[2] // 2
        return jnp.concatenate(
            [amps_ref[:, j, h * part:(h + 1) * part].reshape(cols // 2, cols) for h in range(2)], axis=0
        )

    put(0, whole(0))
    put(2, whole(2).T)
    put(3, whole(3))

    @pl.when(parity == 0)
    def _():
        put(1, halves(1).T)
        put(4, halves(4))

    @pl.when(parity == 1)
    def _():
        put(1, halves(1))
        put(4, halves(4).T)

    tile = rows // sems.shape[0]
    copies = []
    for j in range(sems.shape[0]):
        here = pl.ds(j * tile, tile)
        blocks = jnp.concatenate([ref[here, :] for ref in (o_ref, p_ref, f_ref, s_ref, x_ref)], axis=1)
        result[here, :] = keep_rows(mm(blocks, weights[...]), j * tile, aux_ref[g]).astype(result.dtype)
        copy = pltpu.make_async_copy(result.at[here, :], out_ref.at[here, :], sems.at[j])
        copy.start()
        copies.append(copy)
    for copy in copies:
        copy.wait()


def cost(flops, size):
    return pl.CostEstimate(flops=flops, bytes_accessed=size, transcendentals=0)


def memory(mebibytes):
    return pltpu.CompilerParams(vmem_limit_bytes=mebibytes << 20)


def per_device(three_index, occ_energy, vir_energy, aux_count, occ_count):
    rows, cols = three_index.shape
    nv = vir_energy.shape[0]
    slabs = lax.axis_size("blk")
    owners = lax.axis_size("grp")
    piece = cols // owners
    part = piece // 2

    def across(value, steps):
        pairs = [(i, (i + (steps if i % 2 == 0 else -steps)) % slabs) for i in range(slabs)]
        return lax.ppermute(value, "blk", pairs)

    def swap(value):
        return lax.ppermute(value, "blk", [(i, i ^ 1) for i in range(slabs)])

    def shape(*dims, dtype=BF):
        return jax.ShapeDtypeStruct(dims, dtype)

    own = three_index
    f_block = across(own, -2)
    partner = swap(own)
    partner_energy = swap(occ_energy)

    ot, pt, near, gaps, head = pl.pallas_call(
        prep_kernel,
        in_specs=[SM, SM, SM, VM, VM, VM, VM],
        out_specs=[VM] * 5,
        out_shape=[
            shape(cols, rows), shape(cols, rows), shape(owners, piece + part, cols),
            shape(8 + piece + part, cols, dtype=F32), shape(16, cols),
        ],
        cost_estimate=cost(3 * rows * cols * cols, 8 * rows * cols),
        compiler_params=memory(20),
        name="prep",
    )(
        aux_count, occ_energy, partner_energy, vir_energy[None, :],
        jnp.broadcast_to(vir_energy[:, None], (nv, cols)), own, partner,
    )
    own_later, near = lax.optimization_barrier((own, near))
    s_block = across(own_later, 2)
    parts = shape(owners, 3 * piece, cols)
    partial_sums = pl.pallas_call(
        far_kernel,
        in_specs=[VM] * 4,
        out_specs=VM,
        out_shape=parts,
        cost_estimate=cost(3 * rows * cols * cols, 5 * rows * cols),
        compiler_params=memory(12),
        name="far",
    )(f_block, ot, pt, near)
    pieces = lax.all_to_all(partial_sums, "grp", 0, 0)
    pieces, s_block = lax.optimization_barrier((pieces, s_block))
    sums, message, extra = pl.pallas_call(
        pack_kernel,
        in_specs=[VM, VM],
        out_specs=[VM] * 3,
        out_shape=[
            shape(2 * piece + part, cols, dtype=F32), shape(piece + part + 16, cols), shape(piece, cols),
        ],
        cost_estimate=cost(cols * cols, 4 * cols * cols),
        compiler_params=memory(6),
        name="pack",
    )(pieces, head)
    message, energy = lax.optimization_barrier((message, occ_energy))
    f_energy = across(energy, -2)
    fifth = swap(f_block)
    message = across(message, 2)
    extra = swap(extra)
    amps = pl.pallas_call(
        lambda *refs: amplitude_kernel(nv, *refs),
        in_specs=[SM, SM] + [VM] * 4,
        out_specs=VM,
        out_shape=shape(owners, 5, piece, cols),
        cost_estimate=cost(cols * cols, 8 * cols * cols),
        compiler_params=memory(6),
        name="amplitude",
    )(occ_count, f_energy, sums, gaps, message, extra)
    amps, fifth = lax.optimization_barrier((amps, fifth))
    amps = lax.all_to_all(amps, "grp", 0, 0)

    tiles = 8
    return pl.pallas_call(
        gamma_kernel,
        in_specs=[SM] + [VM] * 6,
        out_specs=ANY,
        out_shape=jax.ShapeDtypeStruct((rows, cols), three_index.dtype),
        scratch_shapes=[
            pltpu.VMEM((rows, cols), three_index.dtype), pltpu.VMEM((5 * cols, cols), BF),
            pltpu.SemaphoreType.DMA((tiles,)),
        ],
        cost_estimate=cost(10 * rows * cols * cols, 14 * rows * cols),
        compiler_params=memory(20),
        name="gamma",
    )(aux_count, amps, own, partner, f_block, s_block, fifth)


def solution(mesh):
    in_specs = (P("grp", "blk"), P("blk"), P(), P(), P())
    out_specs = P("grp", "blk")
    return jax.shard_map(
        per_device, mesh=mesh, in_specs=in_specs, out_specs=out_specs, check_vma=False
    )
```

```python
import jax
import jax.numpy as jnp
from jax import lax
from jax.experimental import pallas as pl
from jax.experimental.pallas import tpu as pltpu
from jax.sharding import PartitionSpec as P


BF = jnp.bfloat16
F32 = jnp.float32
VM = pl.BlockSpec(memory_space=pltpu.VMEM)
SM = pl.BlockSpec(memory_space=pltpu.SMEM)
ANY = pl.BlockSpec(memory_space=pl.ANY)


def mm(a, b):
    return jnp.dot(a, b, preferred_element_type=F32)


def keep_rows(block, start, count):
    row = lax.broadcasted_iota(jnp.int32, block.shape, 0) + start
    return jnp.where(row < count, block, jnp.zeros((), block.dtype))


def place():
    r = lax.axis_index("blk")
    return r, lax.rem(r, 2), lax.axis_index("grp")


def at(count_ref, index):
    slabs = count_ref.shape[0]
    return count_ref[lax.rem(index + slabs, slabs)]


def three_terms(value):
    hi = value.astype(BF)
    rest = value - hi.astype(F32)
    mid = rest.astype(BF)
    low = (rest - mid.astype(F32)).astype(BF)
    return [hi.astype(F32), mid.astype(F32), low.astype(F32)]


def prep_kernel(
    aux_ref, energy_ref, other_ref, vir_ref, vir_rows_ref, own_ref, p_ref,
    ot_ref, pt_ref, near_ref, gaps_ref, head_ref,
):
    _, parity, g = place()
    cols = own_ref.shape[1]
    middle = cols // 2
    owners = near_ref.shape[0]
    piece = cols // owners
    part = piece // 2
    nv = vir_ref.shape[1]
    count = aux_ref[g]
    ot_ref[...] = keep_rows(own_ref[...], 0, count).T
    pt_ref[...] = keep_rows(p_ref[...], 0, count).T

    def put(rows_of, pair):
        near_ref[:, rows_of] = pair.reshape(owners, pair.shape[0] // owners, cols).astype(BF)

    put(slice(0, piece), mm(ot_ref[...], own_ref[...]))

    @pl.when(parity == 0)
    def _():
        put(slice(piece, piece + part), mm(ot_ref[:middle, :], p_ref[...]))

    @pl.when(parity == 1)
    def _():
        put(slice(piece, piece + part), mm(pt_ref[middle:, :], own_ref[...]))

    slots = cols // nv
    slot = (g * piece) // nv
    k = (g * part) // nv
    vir = jnp.concatenate([vir_ref[...]] * slots, axis=1)

    def spread(value):
        return jnp.broadcast_to(value, (1, cols))

    own_gap = levels(energy_ref, nv, cols) - vir
    other_gap = levels(other_ref, nv, cols) - vir
    own_level = spread(energy_ref[slot])
    own_parts = [energy_ref[k], energy_ref[k + slots // 2]]
    other_parts = [other_ref[k], other_ref[k + slots // 2]]
    even_parts = [jnp.where(parity == 0, a, b) for a, b in zip(own_parts, other_parts)]
    terms = []
    for row in [own_gap, other_gap, own_level] + [spread(value) for value in other_parts]:
        terms += three_terms(row)
    head_ref[...] = jnp.concatenate(terms + [jnp.zeros((1, cols), F32)], axis=0).astype(BF)
    gaps_ref[0:8, :] = jnp.concatenate(
        [own_gap, other_gap, own_level, vir] + [spread(value) for value in even_parts + own_parts], axis=0
    )
    start = pl.multiple_of(lax.rem(g * piece, nv), piece)
    gaps_ref[8:8 + piece, :] = vir_rows_ref[pl.ds(start, piece), :]
    start = pl.multiple_of(lax.rem(g * part, nv), part)
    gaps_ref[8 + piece:, :] = vir_rows_ref[pl.ds(start, part), :]


def levels(energy_ref, nv, cols):
    lane = lax.broadcasted_iota(jnp.int32, (1, cols), 1)
    level = jnp.zeros((1, cols), F32)
    for k in range(cols // nv):
        level = jnp.where(lane // nv == k, energy_ref[k], level)
    return level


def far_kernel(f_ref, ot_ref, pt_ref, near_ref, out_ref):
    _, parity, _ = place()
    owners, _, cols = out_ref.shape
    middle = cols // 2
    near = near_ref.shape[1]
    piece = cols // owners
    out_ref[:, 0:near] = near_ref[...]
    out_ref[:, near:near + piece] = mm(ot_ref[...], f_ref[...]).reshape(owners, piece, cols).astype(BF)

    def put(pair):
        out_ref[:, near + piece:] = pair.reshape(owners, piece // 2, cols).astype(BF)

    @pl.when(parity == 0)
    def _():
        put(mm(pt_ref[:middle, :], f_ref[...]))

    @pl.when(parity == 1)
    def _():
        put(mm(pt_ref[...], f_ref[:, middle:]).T)


def pack_kernel(parts_ref, head_ref, sum_ref, message_ref, swap_ref):
    total = jnp.sum(parts_ref[...].astype(F32), axis=0)
    size = parts_ref.shape[2] // parts_ref.shape[0]
    part = size // 2
    near = size + part
    across = total[near + size:].astype(BF)
    sum_ref[...] = total[:near + size]
    message_ref[0:size, :] = total[near:near + size].astype(BF)
    message_ref[size:near, :] = across
    message_ref[near:, :] = head_ref[...]
    swap_ref[0:part, :] = across
    swap_ref[part:, :] = total[size:near].astype(BF)


def amplitude_kernel(nv, count_ref, energy_ref, sum_ref, gaps_ref, message_ref, swap_ref, out_ref):
    r, parity, g = place()
    owners, _, size, cols = out_ref.shape
    part = size // 2
    near = size + part
    slot = (g * size) // nv
    sign = 1 - 2 * parity
    vir = gaps_ref[8:8 + size, :]
    vir_part = gaps_ref[8 + size:, :]
    own_gap = gaps_ref[0:1, :]
    own_rows = gaps_ref[2:3, :] - vir
    own_count, p_count = count_ref[r], count_ref[r + sign]
    f_count, s_count, x_count = at(count_ref, r + 2 * sign), at(count_ref, r - 2 * sign), at(count_ref, r - sign)
    lane = lax.broadcasted_iota(jnp.int32, (size, cols), 1)

    def head(row):
        block = message_ref[near:, :].astype(F32)
        return block[3 * row:3 * row + 1] + block[3 * row + 1:3 * row + 2] + block[3 * row + 2:3 * row + 3]

    def put(j, rows, pair, gap_rows, gap_cols, row_live, col_count):
        keep = (lane[:pair.shape[0]] < col_count * nv) & row_live
        amp = jnp.where(keep, pair / (gap_rows + gap_cols), 0.0).astype(BF)
        for owner in range(owners):
            out_ref[owner, j, rows] = amp

    every = slice(0, size)
    put(0, every, sum_ref[0:size, :], own_rows, own_gap, slot < own_count, own_count)
    f_gap = levels(energy_ref, nv, cols) - gaps_ref[3:4, :]
    put(2, every, sum_ref[near:, :], own_rows, f_gap, slot < own_count, f_count)
    put(3, every, message_ref[0:size, :].astype(F32), head(2) - vir, own_gap, slot < s_count, own_count)

    even = parity == 0
    even_count, odd_count = jnp.where(even, own_count, p_count), jnp.where(even, p_count, own_count)
    odd_gap = jnp.where(even, gaps_ref[1:2, :], own_gap)
    row_count, col_count = jnp.where(even, x_count, own_count), jnp.where(even, own_count, x_count)
    col_gap = jnp.where(even, own_gap, head(1))
    for h in range(2):
        k = (g * part) // nv + h * (cols // nv // 2)
        rows = slice(h * part, (h + 1) * part)
        pair = jnp.where(parity == h, sum_ref[size:near, :], swap_ref[part:, :].astype(F32))
        put(1, rows, pair, gaps_ref[4 + h:5 + h, :] - vir_part, odd_gap, k < even_count, odd_count)
        pair = jnp.where(parity == h, message_ref[size:near, :].astype(F32), swap_ref[0:part, :].astype(F32))
        level = jnp.where(even, head(3 + h), gaps_ref[6 + h:7 + h, :])
        put(4, rows, pair, level - vir_part, col_gap, k < row_count, col_count)


def gamma_kernel(aux_ref, amps_ref, o_ref, p_ref, f_ref, s_ref, x_ref, out_ref, result, weights, sems):
    rows, cols = o_ref.shape
    _, parity, g = place()

    def put(j, matrix):
        weights[j * cols:(j + 1) * cols, :] = matrix

    def whole(j):
        return amps_ref[:, j].reshape(cols, cols)

    def halves(j):
        part = amps_ref.shape[2] // 2
        return jnp.concatenate(
            [amps_ref[:, j, h * part:(h + 1) * part].reshape(cols // 2, cols) for h in range(2)], axis=0
        )

    put(0, whole(0))
    put(2, whole(2).T)
    put(3, whole(3))

    @pl.when(parity == 0)
    def _():
        put(1, halves(1).T)
        put(4, halves(4))

    @pl.when(parity == 1)
    def _():
        put(1, halves(1))
        put(4, halves(4).T)

    tile = rows // sems.shape[0]
    copies = []
    for j in range(sems.shape[0]):
        here = pl.ds(j * tile, tile)
        blocks = jnp.concatenate([ref[here, :] for ref in (o_ref, p_ref, f_ref, s_ref, x_ref)], axis=1)
        result[here, :] = keep_rows(mm(blocks, weights[...]), j * tile, aux_ref[g]).astype(result.dtype)
        copy = pltpu.make_async_copy(result.at[here, :], out_ref.at[here, :], sems.at[j])
        copy.start()
        copies.append(copy)
    for copy in copies:
        copy.wait()


def cost(flops, size):
    return pl.CostEstimate(flops=flops, bytes_accessed=size, transcendentals=0)


def memory(mebibytes):
    return pltpu.CompilerParams(vmem_limit_bytes=mebibytes << 20)


def per_device(three_index, occ_energy, vir_energy, aux_count, occ_count):
    rows, cols = three_index.shape
    nv = vir_energy.shape[0]
    slabs = lax.axis_size("blk")
    owners = lax.axis_size("grp")
    piece = cols // owners
    part = piece // 2

    def across(value, steps):
        pairs = [(i, (i + (steps if i % 2 == 0 else -steps)) % slabs) for i in range(slabs)]
        return lax.ppermute(value, "blk", pairs)

    def swap(value):
        return lax.ppermute(value, "blk", [(i, i ^ 1) for i in range(slabs)])

    def shape(*dims, dtype=BF):
        return jax.ShapeDtypeStruct(dims, dtype)

    own = three_index
    f_block = across(own, -2)
    partner = swap(own)
    partner_energy = swap(occ_energy)
    f_energy = across(occ_energy, -2)

    ot, pt, near, gaps, head = pl.pallas_call(
        prep_kernel,
        in_specs=[SM, SM, SM, VM, VM, VM, VM],
        out_specs=[VM] * 5,
        out_shape=[
            shape(cols, rows), shape(cols, rows), shape(owners, piece + part, cols),
            shape(8 + piece + part, cols, dtype=F32), shape(16, cols),
        ],
        cost_estimate=cost(3 * rows * cols * cols, 8 * rows * cols),
        compiler_params=memory(20),
        name="prep",
    )(
        aux_count, occ_energy, partner_energy, vir_energy[None, :],
        jnp.broadcast_to(vir_energy[:, None], (nv, cols)), own, partner,
    )
    own_later, near, f_energy = lax.optimization_barrier((own, near, f_energy))
    s_block = across(own_later, 2)
    parts = shape(owners, 3 * piece, cols)
    partial_sums = pl.pallas_call(
        far_kernel,
        in_specs=[VM] * 4,
        out_specs=VM,
        out_shape=parts,
        cost_estimate=cost(3 * rows * cols * cols, 5 * rows * cols),
        compiler_params=memory(12),
        name="far",
    )(f_block, ot, pt, near)
    pieces = lax.all_to_all(partial_sums, "grp", 0, 0)
    sums, message, extra = pl.pallas_call(
        pack_kernel,
        in_specs=[VM, VM],
        out_specs=[VM] * 3,
        out_shape=[
            shape(2 * piece + part, cols, dtype=F32), shape(piece + part + 16, cols), shape(piece, cols),
        ],
        cost_estimate=cost(cols * cols, 4 * cols * cols),
        compiler_params=memory(6),
        name="pack",
    )(pieces, head)
    fifth = swap(f_block)
    message, s_block, fifth = lax.optimization_barrier((message, s_block, fifth))
    message = across(message, 2)
    extra = swap(extra)
    amps = pl.pallas_call(
        lambda *refs: amplitude_kernel(nv, *refs),
        in_specs=[SM, SM] + [VM] * 4,
        out_specs=VM,
        out_shape=shape(owners, 5, piece, cols),
        cost_estimate=cost(cols * cols, 8 * cols * cols),
        compiler_params=memory(6),
        name="amplitude",
    )(occ_count, f_energy, sums, gaps, message, extra)
    amps = lax.all_to_all(amps, "grp", 0, 0)

    tiles = 4
    return pl.pallas_call(
        gamma_kernel,
        in_specs=[SM] + [VM] * 6,
        out_specs=ANY,
        out_shape=jax.ShapeDtypeStruct((rows, cols), three_index.dtype),
        scratch_shapes=[
            pltpu.VMEM((rows, cols), three_index.dtype), pltpu.VMEM((5 * cols, cols), BF),
            pltpu.SemaphoreType.DMA((tiles,)),
        ],
        cost_estimate=cost(10 * rows * cols * cols, 14 * rows * cols),
        compiler_params=memory(20),
        name="gamma",
    )(aux_count, amps, own, partner, f_block, s_block, fifth)


def solution(mesh):
    in_specs = (P("grp", "blk"), P("blk"), P(), P(), P())
    out_specs = P("grp", "blk")
    return jax.shard_map(
        per_device, mesh=mesh, in_specs=in_specs, out_specs=out_specs, check_vma=False
    )
```

```python
import jax
import jax.numpy as jnp
from jax import lax
from jax.experimental import pallas as pl
from jax.experimental.pallas import tpu as pltpu
from jax.sharding import PartitionSpec as P


BF = jnp.bfloat16
F32 = jnp.float32
VM = pl.BlockSpec(memory_space=pltpu.VMEM)
SM = pl.BlockSpec(memory_space=pltpu.SMEM)
ANY = pl.BlockSpec(memory_space=pl.ANY)


def mm(a, b):
    return jnp.dot(a, b, preferred_element_type=F32)


def keep_rows(block, start, count):
    row = lax.broadcasted_iota(jnp.int32, block.shape, 0) + start
    return jnp.where(row < count, block, jnp.zeros((), block.dtype))


def place():
    r = lax.axis_index("blk")
    return r, lax.rem(r, 2), lax.axis_index("grp")


def at(count_ref, index):
    slabs = count_ref.shape[0]
    return count_ref[lax.rem(index + slabs, slabs)]


def three_terms(value):
    hi = value.astype(BF)
    rest = value - hi.astype(F32)
    mid = rest.astype(BF)
    low = (rest - mid.astype(F32)).astype(BF)
    return [hi.astype(F32), mid.astype(F32), low.astype(F32)]


def prep_kernel(
    aux_ref, energy_ref, other_ref, vir_ref, vir_rows_ref, own_ref, p_ref,
    ot_ref, pt_ref, near_ref, gaps_ref, head_ref,
):
    _, parity, g = place()
    cols = own_ref.shape[1]
    middle = cols // 2
    owners = near_ref.shape[0]
    piece = cols // owners
    part = piece // 2
    nv = vir_ref.shape[1]
    count = aux_ref[g]
    ot_ref[...] = keep_rows(own_ref[...], 0, count).T
    pt_ref[...] = keep_rows(p_ref[...], 0, count).T

    def put(rows_of, pair):
        near_ref[:, rows_of] = pair.reshape(owners, pair.shape[0] // owners, cols).astype(BF)

    put(slice(0, piece), mm(ot_ref[...], own_ref[...]))

    @pl.when(parity == 0)
    def _():
        put(slice(piece, piece + part), mm(ot_ref[:middle, :], p_ref[...]))

    @pl.when(parity == 1)
    def _():
        put(slice(piece, piece + part), mm(pt_ref[middle:, :], own_ref[...]))

    slots = cols // nv
    slot = (g * piece) // nv
    k = (g * part) // nv
    vir = jnp.concatenate([vir_ref[...]] * slots, axis=1)

    def spread(value):
        return jnp.broadcast_to(value, (1, cols))

    own_gap = levels(energy_ref, nv, cols) - vir
    other_gap = levels(other_ref, nv, cols) - vir
    own_level = spread(energy_ref[slot])
    own_parts = [energy_ref[k], energy_ref[k + slots // 2]]
    other_parts = [other_ref[k], other_ref[k + slots // 2]]
    even_parts = [jnp.where(parity == 0, a, b) for a, b in zip(own_parts, other_parts)]
    terms = []
    for row in [own_gap, other_gap, own_level] + [spread(value) for value in other_parts]:
        terms += three_terms(row)
    head_ref[...] = jnp.concatenate(terms + [jnp.zeros((1, cols), F32)], axis=0).astype(BF)
    gaps_ref[0:8, :] = jnp.concatenate(
        [own_gap, other_gap, own_level, vir] + [spread(value) for value in even_parts + own_parts], axis=0
    )
    start = pl.multiple_of(lax.rem(g * piece, nv), piece)
    gaps_ref[8:8 + piece, :] = vir_rows_ref[pl.ds(start, piece), :]
    start = pl.multiple_of(lax.rem(g * part, nv), part)
    gaps_ref[8 + piece:, :] = vir_rows_ref[pl.ds(start, part), :]


def levels(energy_ref, nv, cols):
    lane = lax.broadcasted_iota(jnp.int32, (1, cols), 1)
    level = jnp.zeros((1, cols), F32)
    for k in range(cols // nv):
        level = jnp.where(lane // nv == k, energy_ref[k], level)
    return level


def far_kernel(f_ref, ot_ref, pt_ref, near_ref, out_ref):
    _, parity, _ = place()
    owners, _, cols = out_ref.shape
    middle = cols // 2
    near = near_ref.shape[1]
    piece = cols // owners
    out_ref[:, 0:near] = near_ref[...]
    out_ref[:, near:near + piece] = mm(ot_ref[...], f_ref[...]).reshape(owners, piece, cols).astype(BF)

    def put(pair):
        out_ref[:, near + piece:] = pair.reshape(owners, piece // 2, cols).astype(BF)

    @pl.when(parity == 0)
    def _():
        put(mm(pt_ref[:middle, :], f_ref[...]))

    @pl.when(parity == 1)
    def _():
        put(mm(pt_ref[...], f_ref[:, middle:]).T)


def pack_kernel(parts_ref, head_ref, sum_ref, message_ref, swap_ref):
    total = jnp.sum(parts_ref[...].astype(F32), axis=0)
    size = parts_ref.shape[2] // parts_ref.shape[0]
    part = size // 2
    near = size + part
    across = total[near + size:].astype(BF)
    sum_ref[...] = total[:near + size]
    message_ref[0:size, :] = total[near:near + size].astype(BF)
    message_ref[size:near, :] = across
    message_ref[near:, :] = head_ref[...]
    swap_ref[0:part, :] = across
    swap_ref[part:, :] = total[size:near].astype(BF)


def amplitude_kernel(nv, count_ref, energy_ref, sum_ref, gaps_ref, message_ref, swap_ref, out_ref):
    r, parity, g = place()
    owners, _, size, cols = out_ref.shape
    part = size // 2
    near = size + part
    slot = (g * size) // nv
    sign = 1 - 2 * parity
    vir = gaps_ref[8:8 + size, :]
    vir_part = gaps_ref[8 + size:, :]
    own_gap = gaps_ref[0:1, :]
    own_rows = gaps_ref[2:3, :] - vir
    own_count, p_count = count_ref[r], count_ref[r + sign]
    f_count, s_count, x_count = at(count_ref, r + 2 * sign), at(count_ref, r - 2 * sign), at(count_ref, r - sign)
    lane = lax.broadcasted_iota(jnp.int32, (size, cols), 1)

    def head(row):
        block = message_ref[near:, :].astype(F32)
        return block[3 * row:3 * row + 1] + block[3 * row + 1:3 * row + 2] + block[3 * row + 2:3 * row + 3]

    def put(j, rows, pair, gap_rows, gap_cols, row_live, col_count):
        keep = (lane[:pair.shape[0]] < col_count * nv) & row_live
        amp = jnp.where(keep, pair / (gap_rows + gap_cols), 0.0).astype(BF)
        for owner in range(owners):
            out_ref[owner, j, rows] = amp

    every = slice(0, size)
    put(0, every, sum_ref[0:size, :], own_rows, own_gap, slot < own_count, own_count)
    f_gap = levels(energy_ref, nv, cols) - gaps_ref[3:4, :]
    put(2, every, sum_ref[near:, :], own_rows, f_gap, slot < own_count, f_count)
    put(3, every, message_ref[0:size, :].astype(F32), head(2) - vir, own_gap, slot < s_count, own_count)

    even = parity == 0
    even_count, odd_count = jnp.where(even, own_count, p_count), jnp.where(even, p_count, own_count)
    odd_gap = jnp.where(even, gaps_ref[1:2, :], own_gap)
    row_count, col_count = jnp.where(even, x_count, own_count), jnp.where(even, own_count, x_count)
    col_gap = jnp.where(even, own_gap, head(1))
    for h in range(2):
        k = (g * part) // nv + h * (cols // nv // 2)
        rows = slice(h * part, (h + 1) * part)
        pair = jnp.where(parity == h, sum_ref[size:near, :], swap_ref[part:, :].astype(F32))
        put(1, rows, pair, gaps_ref[4 + h:5 + h, :] - vir_part, odd_gap, k < even_count, odd_count)
        pair = jnp.where(parity == h, message_ref[size:near, :].astype(F32), swap_ref[0:part, :].astype(F32))
        level = jnp.where(even, head(3 + h), gaps_ref[6 + h:7 + h, :])
        put(4, rows, pair, level - vir_part, col_gap, k < row_count, col_count)


def gamma_kernel(aux_ref, amps_ref, o_ref, p_ref, f_ref, s_ref, x_ref, out_ref, result, weights, sems):
    rows, cols = o_ref.shape
    _, parity, g = place()

    def put(j, matrix):
        weights[j * cols:(j + 1) * cols, :] = matrix

    def whole(j):
        return amps_ref[:, j].reshape(cols, cols)

    def halves(j):
        part = amps_ref.shape[2] // 2
        return jnp.concatenate(
            [amps_ref[:, j, h * part:(h + 1) * part].reshape(cols // 2, cols) for h in range(2)], axis=0
        )

    put(0, whole(0))
    put(2, whole(2).T)
    put(3, whole(3))

    @pl.when(parity == 0)
    def _():
        put(1, halves(1).T)
        put(4, halves(4))

    @pl.when(parity == 1)
    def _():
        put(1, halves(1))
        put(4, halves(4).T)

    tile = rows // sems.shape[0]
    copies = []
    for j in range(sems.shape[0]):
        here = pl.ds(j * tile, tile)
        blocks = jnp.concatenate([ref[here, :] for ref in (o_ref, p_ref, f_ref, s_ref, x_ref)], axis=1)
        result[here, :] = keep_rows(mm(blocks, weights[...]), j * tile, aux_ref[g]).astype(result.dtype)
        copy = pltpu.make_async_copy(result.at[here, :], out_ref.at[here, :], sems.at[j])
        copy.start()
        copies.append(copy)
    for copy in copies:
        copy.wait()


def cost(flops, size):
    return pl.CostEstimate(flops=flops, bytes_accessed=size, transcendentals=0)


def memory(mebibytes):
    return pltpu.CompilerParams(vmem_limit_bytes=mebibytes << 20)


def per_device(three_index, occ_energy, vir_energy, aux_count, occ_count):
    rows, cols = three_index.shape
    nv = vir_energy.shape[0]
    slabs = lax.axis_size("blk")
    owners = lax.axis_size("grp")
    piece = cols // owners
    part = piece // 2

    def across(value, steps):
        pairs = [(i, (i + (steps if i % 2 == 0 else -steps)) % slabs) for i in range(slabs)]
        return lax.ppermute(value, "blk", pairs)

    def swap(value):
        return lax.ppermute(value, "blk", [(i, i ^ 1) for i in range(slabs)])

    def shape(*dims, dtype=BF):
        return jax.ShapeDtypeStruct(dims, dtype)

    own = three_index
    f_block = across(own, -2)
    partner = swap(own)
    partner_energy = swap(occ_energy)
    f_energy = across(occ_energy, -2)

    ot, pt, near, gaps, head = pl.pallas_call(
        prep_kernel,
        in_specs=[SM, SM, SM, VM, VM, VM, VM],
        out_specs=[VM] * 5,
        out_shape=[
            shape(cols, rows), shape(cols, rows), shape(owners, piece + part, cols),
            shape(8 + piece + part, cols, dtype=F32), shape(16, cols),
        ],
        cost_estimate=cost(3 * rows * cols * cols, 8 * rows * cols),
        compiler_params=memory(20),
        name="prep",
    )(
        aux_count, occ_energy, partner_energy, vir_energy[None, :],
        jnp.broadcast_to(vir_energy[:, None], (nv, cols)), own, partner,
    )
    own_later, near, f_energy = lax.optimization_barrier((own, near, f_energy))
    s_block = across(own_later, 2)
    parts = shape(owners, 3 * piece, cols)
    partial_sums = pl.pallas_call(
        far_kernel,
        in_specs=[VM] * 4,
        out_specs=VM,
        out_shape=parts,
        cost_estimate=cost(3 * rows * cols * cols, 5 * rows * cols),
        compiler_params=memory(12),
        name="far",
    )(f_block, ot, pt, near)
    pieces = lax.all_to_all(partial_sums, "grp", 0, 0)
    sums, message, extra = pl.pallas_call(
        pack_kernel,
        in_specs=[VM, VM],
        out_specs=[VM] * 3,
        out_shape=[
            shape(2 * piece + part, cols, dtype=F32), shape(piece + part + 16, cols), shape(piece, cols),
        ],
        cost_estimate=cost(cols * cols, 4 * cols * cols),
        compiler_params=memory(6),
        name="pack",
    )(pieces, head)
    message, s_block, f_later = lax.optimization_barrier((message, s_block, f_block))
    message = across(message, 2)
    extra = swap(extra)
    fifth = swap(f_later)
    amps = pl.pallas_call(
        lambda *refs: amplitude_kernel(nv, *refs),
        in_specs=[SM, SM] + [VM] * 4,
        out_specs=VM,
        out_shape=shape(owners, 5, piece, cols),
        cost_estimate=cost(cols * cols, 8 * cols * cols),
        compiler_params=memory(6),
        name="amplitude",
    )(occ_count, f_energy, sums, gaps, message, extra)
    amps, fifth = lax.optimization_barrier((amps, fifth))
    amps = lax.all_to_all(amps, "grp", 0, 0)

    tiles = 8
    return pl.pallas_call(
        gamma_kernel,
        in_specs=[SM] + [VM] * 6,
        out_specs=ANY,
        out_shape=jax.ShapeDtypeStruct((rows, cols), three_index.dtype),
        scratch_shapes=[
            pltpu.VMEM((rows, cols), three_index.dtype), pltpu.VMEM((5 * cols, cols), BF),
            pltpu.SemaphoreType.DMA((tiles,)),
        ],
        cost_estimate=cost(10 * rows * cols * cols, 14 * rows * cols),
        compiler_params=memory(20),
        name="gamma",
    )(aux_count, amps, own, partner, f_block, s_block, fifth)


def solution(mesh):
    in_specs = (P("grp", "blk"), P("blk"), P(), P(), P())
    out_specs = P("grp", "blk")
    return jax.shard_map(
        per_device, mesh=mesh, in_specs=in_specs, out_specs=out_specs, check_vma=False
    )
```
